32 devices in a mesh: rep: 8 (over y, x, core), shard: 4 (over z).
Axes of the slice: x: 2, y: 2, z: 4, core: 2. Of those that a mesh axis runs over, the one named last changes fastest.
Arguments:
- prompt_in: bfloat16 [8, 1024, 2048], P('rep', 'shard'), may hold values from -6 to 6
- cont_in: bfloat16 [8, 8, 96, 2048], P('rep', 'shard'), may hold values from -6 to 6
- cotan_prompt: bfloat16 [8, 1024, 2048], P('rep', 'shard'), may hold values from -6 to 6
- cotan_cont: bfloat16 [8, 8, 96, 2048], P('rep', 'shard'), may hold values from -6 to 6
- routes_attn_p: int32 [8, 1024, 2], P('rep', 'shard'), may hold values from 0 to 3, all different within a row; in each aligned block of 256 rows (0 to 255, 256 to 511, ..., all dimensions but the last counted through in order) at most 136 rows name the same one
- routes_attn_c: int32 [8, 8, 96, 2], P('rep', 'shard'), may hold values from 0 to 3, all different within a row; in each aligned block of 192 rows (0 to 191, 192 to 383, ..., all dimensions but the last counted through in order) at most 104 rows name the same one
- routes_ffn_p: int32 [8, 1024, 2], P('rep', 'shard'), may hold values from 0 to 3, all different within a row; in each aligned block of 256 rows (0 to 255, 256 to 511, ..., all dimensions but the last counted through in order) at most 136 rows name the same one
- routes_ffn_c: int32 [8, 8, 96, 2], P('rep', 'shard'), may hold values from 0 to 3, all different within a row; in each aligned block of 192 rows (0 to 191, 192 to 383, ..., all dimensions but the last counted through in order) at most 104 rows name the same one
- adapter_pick: int32 [8], P('rep'), may hold values from 0 to 7
- norm_gains: bfloat16 [2, 2048], replicated, may hold values from 0.5 to 1.5
- router_attn: bfloat16 [2048, 4], replicated, may hold values from -0.09375 to 0.09375
- router_ffn: bfloat16 [2048, 4], replicated, may hold values from -0.09375 to 0.09375
- w_kv: bfloat16 [2, 2048, 2048], P(None, None, 'shard'), may hold values from -0.125 to 0.125
- w_query: bfloat16 [4, 2048, 2048], P(None, None, 'shard'), may hold values from -0.125 to 0.125
- w_out: bfloat16 [4, 2048, 2048], P(None, None, 'shard'), may hold values from -0.5 to 0.5
- w_gate_up: bfloat16 [4, 2, 2048, 5632], P(None, None, None, 'shard'), may hold values from -0.125 to 0.125
- w_down: bfloat16 [4, 5632, 2048], P(None, 'shard'), may hold values from -0.078125 to 0.078125
- ada_in: bfloat16 [8, 6, 16, 2048], P(None, None, None, 'shard'), may hold values from -0.125 to 0.125
- ada_out: bfloat16 [8, 5, 16, 2048], P(None, None, None, 'shard'), may hold values from -0.75 to 0.75
- ada_down: bfloat16 [8, 16, 5632], P(None, None, 'shard'), may hold values from -0.078125 to 0.078125
- ada_ffn: bfloat16 [8, 2, 16, 5632], P(None, None, None, 'shard'), may hold values from -0.75 to 0.75
Outputs:
- out_prompt: bfloat16 [8, 1024, 2048], P('rep', 'shard')
- out_cont: bfloat16 [8, 8, 96, 2048], P('rep', 'shard')
- grad_prompt: float32 [8, 1024, 2048], P('rep', 'shard')
- grad_cont: float32 [8, 8, 96, 2048], P('rep', 'shard')
- grad_ada_in: float32 [8, 6, 16, 2048], P(None, None, None, 'shard')
- grad_ada_out: float32 [8, 5, 16, 2048], P(None, None, None, 'shard')
- grad_ada_down: float32 [8, 16, 5632], P(None, None, 'shard')
- grad_ada_ffn: float32 [8, 2, 16, 5632], P(None, None, None, 'shard')
The draws below stay inside these ranges and needn't reach their ends.
Inputs may be any that keep to these rules, and one draw needn't show every extreme that they name: `routes_attn_p`: in each aligned block of 256 prompt rows, no attention expert is named by more than 136 rows, a bound that some block reaches; a row names 2 different experts. `routes_attn_c`: in each aligned block of 192 continuation rows, no attention expert is named by more than 104 rows, a bound that some block reaches; a row names 2 different experts. `routes_ffn_p`: in each aligned block of 256 prompt rows, no feed-forward expert is named by more than 136 rows, a bound that some block reaches; a row names 2 different experts. `routes_ffn_c`: in each aligned block of 192 continuation rows, no feed-forward expert is named by more than 104 rows, a bound that some block reaches; a row names 2 different experts.
All inputs are finite; a program needn't handle non-finite values.
Results may differ from the reference program's by a relative error of at most 0.019.
Values may be sent and summed in bfloat16 or wider, within the bound.
No kernel may reach another device: no remote copies, remote signals or barrier semaphores. Data moves between devices by JAX's collectives and lax.ppermute only.
A program may use at most 960 MiB of HBM per device.

```python
import math
import jax
import jax.numpy as jnp
import numpy as np
from jax import lax

D = 2048
HEADS = 16
HD = 128
KVW = 2048
FF = 5632
RANK = 16
A_EXP = 4
F_EXP = 4
TOP = 2
NAD = 8
PROMPT = 1024
CONT = 8
CLEN = 96
GROUPS = 8
PR_DEV = 256
CD_DEV = 2
CAPA_P = 136
CAPA_C = 104
CAPF_P = 136
CAPF_C = 104


def with_ends(entries, key, low, high):
    place = [jax.random.randint(jax.random.fold_in(key, axis), (), 0, length) for axis, length in enumerate(entries.shape)]
    widest = entries.shape.index(max(entries.shape))
    neighbour = place[:widest] + [(place[widest] + 1) % entries.shape[widest]] + place[widest + 1:]
    return entries.at[tuple(place)].set(low).at[tuple(neighbour)].set(high)


def level_of(rng, extent, shards, low, top_value):
    def one(axis_at, blocks):
        draws = jax.random.uniform(jax.random.fold_in(jax.random.fold_in(rng, 6), axis_at), (blocks,), jnp.float32, low / len(shards), top_value / len(shards))
        return jnp.repeat(jnp.exp(draws), extent[axis_at] // blocks).reshape((-1,) + (1,) * (len(extent) - axis_at - 1))

    loudness = one(*shards[0])
    for cut in shards[1:]:
        loudness = loudness * one(*cut)
    return loudness


def assign_block(key, own, number, rows, number_of, top, limit, lean):
    sequence = jax.random.permutation(key, number_of)
    packed, ordinary = load_shares(number_of, rows * top, limit, lean, True), load_shares(number_of, rows * top, limit, lean, False)
    places = jnp.arange(number_of)

    def named(lengths, rotation):
        used = int((lengths > 0).sum())
        fixed = max(1, used // 4)
        moved = fixed + (places - fixed + rotation * (used - fixed)) % max(1, number_of - fixed)
        return jnp.zeros((number_of,), jnp.int32).at[sequence[jnp.where(places < fixed, places, moved)]].set(jnp.asarray(lengths, jnp.int32))

    lengths = jnp.where(number % 4 == 0, named(packed, number // 4), named(ordinary, number - number // 4 - 1))
    mixed = jax.random.permutation(jax.random.fold_in(own, 3), number_of)
    source_of, sink = mixed[0:number_of // 2 * 2:2], mixed[1:number_of // 2 * 2:2]
    slack = jnp.minimum(lengths[source_of] - 1, limit - lengths[sink]) // 2
    slack = jnp.where((source_of == sequence[0]) | (sink == sequence[0]) | (lengths[sink] == 0), 0, jnp.maximum(slack, 0))
    moved = jax.random.randint(jax.random.fold_in(own, 4), (number_of // 2,), 0, 1 << 20) % (slack + 1)
    lengths = lengths.at[source_of].add(-moved).at[sink].add(moved)
    labels = jnp.searchsorted(jnp.cumsum(lengths), jnp.arange(rows * top), side="right").astype(jnp.int32)
    grid = labels.reshape(top, rows).T
    grid = grid[jax.random.permutation(jax.random.fold_in(own, 1), rows)]
    rotation = jax.random.randint(jax.random.fold_in(own, 2), (rows, 1), 0, top)
    return jnp.take_along_axis(grid, (jnp.arange(top)[None, :] + rotation) % top, axis=1)


def load_shares(count, total, bound, slope, full):
    portions = [(1 << 20) // math.isqrt(grade ** slope) + 1 for grade in range(1, count + 1)]
    largest = bound if full else min(bound, max(-(-total // count), total * portions[0] // sum(portions)))
    least = 1 if total - largest >= count - 1 else 0
    counts, rest = [largest] + [least] * (count - 1), total - largest - least * (count - 1)
    while rest > 0:
        free = [i for i in range(1, count) if counts[i] < largest] or [i for i in range(1, count) if counts[i] < bound]
        pool, left = sum([portions[i] for i in free]), rest
        for i in free:
            more = min(bound - counts[i], max(1, left * portions[i] // pool), rest)
            counts[i] = counts[i] + more
            rest = rest - more
    return np.array(counts)


def gaussian(rng, dims, scale, bound, shards=(), kind=jnp.bfloat16):
    drawn = scale * jax.random.normal(rng, dims, jnp.float32)
    if shards:
        drawn = drawn * level_of(rng, dims, shards, -0.22, 0.18)
    return jnp.clip(drawn, -bound, bound).astype(kind)


def setup_inputs(seed: int = 0) -> dict:
    key_of = jax.random.split(jax.random.key(seed), 22)
    prompt_in = gaussian(key_of[0], (GROUPS, PROMPT, D), 1.0, 6.0, ((0, 8), (1, 4)))
    cont_in = gaussian(key_of[1], (GROUPS, CONT, CLEN, D), 1.0, 6.0, ((0, 8), (1, 4)))
    cotan_prompt = gaussian(key_of[2], (GROUPS, PROMPT, D), 1.0, 6.0, ((0, 8), (1, 4)))
    cotan_cont = gaussian(key_of[3], (GROUPS, CONT, CLEN, D), 1.0, 6.0, ((0, 8), (1, 4)))
    routes_attn_p_keys = jax.random.split(jax.random.fold_in(key_of[4], 1), GROUPS * PROMPT // PR_DEV)
    routes_attn_p_turns = jax.random.permutation(jax.random.fold_in(key_of[4], 3), GROUPS * PROMPT // PR_DEV)
    routes_attn_p = jax.vmap(lambda own, number: assign_block(jax.random.fold_in(key_of[4], 2), own, number, PR_DEV, A_EXP, TOP, CAPA_P, 1))(routes_attn_p_keys, routes_attn_p_turns).reshape((GROUPS, PROMPT, TOP))
    routes_attn_c_keys = jax.random.split(jax.random.fold_in(key_of[5], 1), GROUPS * CONT * CLEN // (CD_DEV * CLEN))
    routes_attn_c_turns = jax.random.permutation(jax.random.fold_in(key_of[5], 3), GROUPS * CONT * CLEN // (CD_DEV * CLEN))
    routes_attn_c = jax.vmap(lambda own, number: assign_block(jax.random.fold_in(key_of[5], 2), own, number, CD_DEV * CLEN, A_EXP, TOP, CAPA_C, 1))(routes_attn_c_keys, routes_attn_c_turns).reshape((GROUPS, CONT, CLEN, TOP))
    routes_ffn_p_keys = jax.random.split(jax.random.fold_in(key_of[6], 1), GROUPS * PROMPT // PR_DEV)
    routes_ffn_p_turns = jax.random.permutation(jax.random.fold_in(key_of[6], 3), GROUPS * PROMPT // PR_DEV)
    routes_ffn_p = jax.vmap(lambda own, number: assign_block(jax.random.fold_in(key_of[6], 2), own, number, PR_DEV, F_EXP, TOP, CAPF_P, 1))(routes_ffn_p_keys, routes_ffn_p_turns).reshape((GROUPS, PROMPT, TOP))
    routes_ffn_c_keys = jax.random.split(jax.random.fold_in(key_of[7], 1), GROUPS * CONT * CLEN // (CD_DEV * CLEN))
    routes_ffn_c_turns = jax.random.permutation(jax.random.fold_in(key_of[7], 3), GROUPS * CONT * CLEN // (CD_DEV * CLEN))
    routes_ffn_c = jax.vmap(lambda own, number: assign_block(jax.random.fold_in(key_of[7], 2), own, number, CD_DEV * CLEN, F_EXP, TOP, CAPF_C, 1))(routes_ffn_c_keys, routes_ffn_c_turns).reshape((GROUPS, CONT, CLEN, TOP))
    adapter_pick = with_ends(jax.random.randint(key_of[8], (GROUPS,), 0, NAD), jax.random.fold_in(key_of[8], 1), 0, NAD - 1).astype(jnp.int32)
    norm_gains = jnp.clip(1.0 + 0.1 * jax.random.normal(key_of[9], (2, D), jnp.float32), 0.5, 1.5).astype(jnp.bfloat16)
    router_attn = gaussian(key_of[10], (D, A_EXP), (2 * D) ** -0.5, 0.09375)
    router_ffn = gaussian(key_of[11], (D, F_EXP), (2 * D) ** -0.5, 0.09375)
    w_kv = gaussian(key_of[12], (2, D, KVW), D ** -0.5, 0.125, ((2, 4),))
    w_query = gaussian(key_of[13], (A_EXP, D, KVW), D ** -0.5, 0.125, ((2, 4),))
    w_out = gaussian(key_of[14], (A_EXP, KVW, D), (KVW // 16) ** -0.5, 0.5, ((2, 4),))
    w_gate_up = gaussian(key_of[15], (F_EXP, 2, D, FF), D ** -0.5, 0.125, ((3, 4),))
    w_down = gaussian(key_of[16], (F_EXP, FF, D), FF ** -0.5, 0.078125, ((1, 4),))
    ada_in = gaussian(key_of[17], (NAD, 6, RANK, D), D ** -0.5, 0.125, ((3, 4),))
    ada_out = gaussian(key_of[18], (NAD, 5, RANK, D), (4 * RANK) ** -0.5, 0.75, ((3, 4),))
    ada_down = gaussian(key_of[19], (NAD, RANK, FF), FF ** -0.5, 0.078125, ((2, 4),))
    ada_ffn = gaussian(key_of[20], (NAD, 2, RANK, FF), (4 * RANK) ** -0.5, 0.75, ((3, 4),))
    return dict(prompt_in=prompt_in, cont_in=cont_in, cotan_prompt=cotan_prompt, cotan_cont=cotan_cont, routes_attn_p=routes_attn_p, routes_attn_c=routes_attn_c, routes_ffn_p=routes_ffn_p, routes_ffn_c=routes_ffn_c, adapter_pick=adapter_pick, norm_gains=norm_gains, router_attn=router_attn, router_ffn=router_ffn, w_kv=w_kv, w_query=w_query, w_out=w_out, w_gate_up=w_gate_up, w_down=w_down, ada_in=ada_in, ada_out=ada_out, ada_down=ada_down, ada_ffn=ada_ffn)


@jax.custom_vjp
def low(v):
    return lax.optimization_barrier(v.astype(jnp.bfloat16)).astype(jnp.float32)

@jax.custom_vjp
def low_back(v):
    return v

def low_keep(v):
    return (low(v), None)

def low_pass(kept, grad):
    return (grad,)

def back_keep(v):
    return (v, None)

def back_low(kept, grad):
    return (low(grad),)
low.defvjp(low_keep, low_pass)
low_back.defvjp(back_keep, back_low)
EPSILON = 1e-05
HIGHEST = lax.Precision.HIGHEST

def norm_rows(values, scaling):
    return values * lax.rsqrt(lax.optimization_barrier(jnp.mean(values * values, axis=-1, keepdims=True)) + EPSILON) * scaling

def exact_mm(former, latter):
    return jnp.dot(former, latter, precision=HIGHEST)

def route_weights(logits, routes, experts):
    chosen = jnp.take_along_axis(logits, routes, axis=1)
    shares = jax.nn.softmax(chosen, axis=-1)
    onehot = (routes[:, :, None] == jnp.arange(experts, dtype=jnp.int32)[None, None, :]).astype(shares.dtype)
    return jnp.einsum('nk,nke->ne', shares, onehot, precision=HIGHEST)

def layer_forward(tokens, seq_ids, routes_attn, routes_ffn, frozen, chosen):
    gains, router_attn, router_ffn, w_kv, w_query, w_out, w_gate_up, w_down = frozen
    a_in, a_out, a_down, a_ffn = chosen
    amount = tokens.shape[0]
    normed = low(norm_rows(tokens, gains[0]))
    gate_attn = route_weights(exact_mm(normed, router_attn), routes_attn, A_EXP)
    low_in = jnp.einsum('nd,jrd->njr', normed, a_in[:3], precision=HIGHEST)
    kv_rows = jnp.einsum('nd,jdk->njk', normed, w_kv, precision=HIGHEST) + jnp.einsum('njr,jrk->njk', low_in[:, 1:3], a_out[1:3], precision=HIGHEST)
    kv_rows = low_back(low(kv_rows))
    key_rows = kv_rows[:, 0].reshape(amount, HEADS, HD)
    value_rows = kv_rows[:, 1].reshape(amount, HEADS, HD)
    positions = jnp.arange(amount, dtype=jnp.int32)
    same_seq = (seq_ids[None, :] == 0) | (seq_ids[None, :] == seq_ids[:, None])
    allowed = same_seq & (positions[None, :] <= positions[:, None])
    query_shift = exact_mm(low_in[:, 0], a_out[0])

    def attend_expert(weights):
        w_q_one, w_o_one = weights
        queries = low_back(low(exact_mm(normed, w_q_one) + query_shift)).reshape(amount, HEADS, HD)
        scores = low_back(jnp.einsum('shd,khd->hsk', queries, key_rows, precision=HIGHEST) * HD ** (-0.5))
        scores = jnp.where(allowed[None], scores, -1e+30)
        prob_rows = low(jax.nn.softmax(scores, axis=-1))
        mixture = jnp.einsum('hsk,khd->shd', prob_rows, value_rows, precision=HIGHEST).reshape(amount, HEADS * HD)
        mixture = low_back(low(mixture))
        return low_back(exact_mm(mixture, w_o_one) + exact_mm(exact_mm(mixture, a_in[3].T), a_out[3]))
    branch = lax.map(jax.checkpoint(attend_expert), (w_query, w_out))
    hidden_one = tokens + jnp.einsum('ne,end->nd', gate_attn, branch, precision=HIGHEST)
    normed_two = low(norm_rows(hidden_one, gains[1]))
    gate_ffn = route_weights(exact_mm(normed_two, router_ffn), routes_ffn, F_EXP)
    low_ff = jnp.einsum('nd,jrd->njr', normed_two, a_in[4:6], precision=HIGHEST)
    ff_shift = jnp.einsum('njr,jrf->njf', low_ff, a_ffn, precision=HIGHEST)

    def ffn_expert(weights):
        w_gu_one, w_down_one = weights
        gate_up = low_back(jnp.einsum('nd,jdf->njf', normed_two, w_gu_one, precision=HIGHEST) + ff_shift)
        activated = low(jax.nn.silu(gate_up[:, 0]) * gate_up[:, 1])
        return low_back(exact_mm(activated, w_down_one) + exact_mm(exact_mm(activated, a_down.T), a_out[4]))
    expert_out = lax.map(jax.checkpoint(ffn_expert), (w_gate_up, w_down))
    return hidden_one + jnp.einsum('ne,end->nd', gate_ffn, expert_out, precision=HIGHEST)

def reference(prompt_in, cont_in, cotan_prompt, cotan_cont, routes_attn_p, routes_attn_c, routes_ffn_p, routes_ffn_c, adapter_pick, norm_gains, router_attn, router_ffn, w_kv, w_query, w_out, w_gate_up, w_down, ada_in, ada_out, ada_down, ada_ffn):
    frozen = tuple((member.astype(jnp.float32) for member in (norm_gains, router_attn, router_ffn, w_kv, w_query, w_out, w_gate_up, w_down)))
    adapters = tuple((member.astype(jnp.float32) for member in (ada_in, ada_out, ada_down, ada_ffn)))
    seq_ids = jnp.concatenate([jnp.zeros((PROMPT,), jnp.int32), jnp.repeat(jnp.arange(1, CONT + 1, dtype=jnp.int32), CLEN)])

    def one_group(totals, element):
        part_p, part_c, cot_p, cot_c, attn_p, attn_c, ffn_p, ffn_c, chosen_id = element
        tokens = jnp.concatenate([part_p, part_c.reshape(CONT * CLEN, D)], axis=0).astype(jnp.float32)
        cotangent = jnp.concatenate([cot_p, cot_c.reshape(CONT * CLEN, D)], axis=0).astype(jnp.float32)
        routes_attn = jnp.concatenate([attn_p, attn_c.reshape(CONT * CLEN, TOP)], axis=0)
        routes_ffn = jnp.concatenate([ffn_p, ffn_c.reshape(CONT * CLEN, TOP)], axis=0)

        def forward(token_rows, a_in, a_out, a_down, a_ffn):
            chosen = tuple((lax.dynamic_index_in_dim(member, chosen_id, 0, keepdims=False) for member in (a_in, a_out, a_down, a_ffn)))
            return layer_forward(token_rows, seq_ids, routes_attn, routes_ffn, frozen, chosen)
        result, pullback = jax.vjp(forward, tokens, *adapters)
        gradients = pullback(cotangent)
        totals = tuple((former + latter for former, latter in zip(totals, gradients[1:])))
        return (totals, (result.astype(jnp.bfloat16), gradients[0]))
    initial = tuple((jnp.zeros_like(member) for member in adapters))
    totals, (results, input_grads) = lax.scan(one_group, initial, (prompt_in, cont_in, cotan_prompt, cotan_cont, routes_attn_p, routes_attn_c, routes_ffn_p, routes_ffn_c, adapter_pick))
    out_prompt = results[:, :PROMPT]
    out_cont = results[:, PROMPT:].reshape(GROUPS, CONT, CLEN, D)
    grad_prompt = input_grads[:, :PROMPT]
    grad_cont = input_grads[:, PROMPT:].reshape(GROUPS, CONT, CLEN, D)
    return (out_prompt, out_cont, grad_prompt, grad_cont, totals[0], totals[1], totals[2], totals[3])
```

```python
import jax
import jax.numpy as jnp
from jax import lax
from jax.sharding import PartitionSpec as P

HD = 128
EPSILON = 1e-05
HIGHEST = lax.Precision.HIGHEST
NEG_FILL = -1e30
F32 = jnp.float32
BF16 = jnp.bfloat16


def dot32(former, latter):
    return jnp.dot(former, latter, preferred_element_type=F32)


def exact_mm(former, latter):
    return jnp.dot(former, latter, precision=HIGHEST)


def norm_rows(values, scaling):
    inverse = lax.rsqrt(jnp.mean(values * values, axis=-1, keepdims=True) + EPSILON)
    return (values * inverse * scaling, inverse)


def norm_back(values, inverse, scaling, upstream):
    weighted = upstream * scaling
    inner_mean = jnp.mean(weighted * values, axis=-1, keepdims=True)
    return inverse * weighted - values * (inverse * inverse * inverse) * inner_mean


def capacity(block_rows, experts, top_count):
    return min(block_rows, ((block_rows * top_count + experts - 1) // experts + 7) // 8 * 8 + 8)


def hits(routes, experts):
    labels = jnp.arange(experts, dtype=jnp.int32)
    return (routes[:, :, None] == labels[None, None, :]).astype(F32)


def slot_onehots(routes, experts, block):
    rows, top_count = routes.shape
    blocks = rows // block
    slot_cap = capacity(block, experts, top_count)
    member = jnp.sum(hits(routes, experts), axis=1).reshape(blocks, block, experts)
    place = jnp.arange(block, dtype=jnp.int32)
    before = (place[None, :] < place[:, None]).astype(BF16)
    ranked = jnp.einsum("rq,bqe->ber", before, member.astype(BF16), preferred_element_type=F32)
    slots = jnp.arange(slot_cap, dtype=F32)
    matched = (ranked[:, :, None, :] == slots[None, None, :, None]) & (
        member.transpose(0, 2, 1)[:, :, None, :] > 0
    )
    return matched.astype(BF16)


def route_shares(logits, routes):
    chosen = jnp.einsum("rte,re->rt", hits(routes, logits.shape[1]), logits, precision=HIGHEST)
    return jax.nn.softmax(chosen, axis=-1)


def shares_back(shares, routes, experts, d_shares):
    d_chosen = shares * (d_shares - jnp.sum(shares * d_shares, axis=-1, keepdims=True))
    return jnp.sum(d_chosen[:, :, None] * hits(routes, experts), axis=1)


def pick_expert(per_expert, routes):
    out = []
    for t in range(routes.shape[1]):
        total = per_expert[0]
        for e in range(1, per_expert.shape[0]):
            total = jnp.where(routes[:, t, None] == e, per_expert[e], total)
        out.append(total)
    return jnp.stack(out)


def spread_expert(per_choice, routes, experts):
    out = []
    for e in range(experts):
        total = jnp.zeros(per_choice.shape[1:], per_choice.dtype)
        for t in range(routes.shape[1]):
            total = jnp.where(routes[:, t, None] == e, per_choice[t], total)
        out.append(total)
    return jnp.concatenate(out, axis=1)


def heads_of(values):
    return values.reshape(values.shape[:-1] + (values.shape[-1] // HD, HD))


def attend_prompt(q, k, v):
    tops, rows, _ = q.shape
    s = jnp.einsum("tqhd,khd->htqk", heads_of(q), heads_of(k), preferred_element_type=F32)
    place = jnp.arange(rows)
    s = jnp.where(place[None, :] <= place[:, None], s * HD**-0.5, NEG_FILL)
    top = jnp.max(s, axis=-1, keepdims=True)
    p = jnp.exp(s - top)
    total = jnp.sum(p, axis=-1, keepdims=True)
    o = jnp.einsum("htqk,khd->tqhd", (p / total).astype(BF16), heads_of(v), preferred_element_type=F32)
    return o.reshape(q.shape).astype(BF16), top + jnp.log(total)


def attend_prompt_back(q, k, v, do, lse):
    rows = q.shape[1]
    qh, kh, vh, gh = (heads_of(m) for m in (q, k, v, do))
    place = jnp.arange(rows)
    s = jnp.einsum("tqhd,khd->htqk", qh, kh, preferred_element_type=F32) * HD**-0.5
    p = jnp.where(place[None, :] <= place[:, None], jnp.exp(s - lse), 0.0)
    dp = jnp.einsum("tqhd,khd->htqk", gh, vh, preferred_element_type=F32)
    ds = (p * (dp - jnp.sum(p * dp, axis=-1, keepdims=True))).astype(BF16)
    dq = jnp.einsum("htqk,khd->tqhd", ds, kh, preferred_element_type=F32) * HD**-0.5
    dk = jnp.einsum("htqk,tqhd->khd", ds, qh, preferred_element_type=F32) * HD**-0.5
    dv = jnp.einsum("htqk,tqhd->khd", p.astype(BF16), gh, preferred_element_type=F32)
    return dq.reshape(q.shape).astype(BF16), dk.reshape(k.shape), dv.reshape(k.shape)


def cont_scores(qh, kph, kch, length):
    s_p = jnp.einsum("tcqhd,khd->htcqk", qh, kph, preferred_element_type=F32) * HD**-0.5
    s_c = jnp.einsum("tcqhd,ckhd->htcqk", qh, kch, preferred_element_type=F32) * HD**-0.5
    place = jnp.arange(length)
    s_c = jnp.where(place[None, :] <= place[:, None], s_c, NEG_FILL)
    return s_p, s_c


def attend_cont(q, kp, vp, kc, vc, length):
    tops, rows, width = q.shape
    conts = rows // length
    qh = heads_of(q.reshape(tops, conts, length, width))
    kch = heads_of(kc.reshape(conts, length, width))
    vch = heads_of(vc.reshape(conts, length, width))
    s_p, s_c = cont_scores(qh, heads_of(kp), kch, length)
    top = jnp.maximum(jnp.max(s_p, axis=-1, keepdims=True), jnp.max(s_c, axis=-1, keepdims=True))
    p_p, p_c = jnp.exp(s_p - top), jnp.exp(s_c - top)
    total = jnp.sum(p_p, axis=-1, keepdims=True) + jnp.sum(p_c, axis=-1, keepdims=True)
    o = jnp.einsum(
        "htcqk,khd->tcqhd", (p_p / total).astype(BF16), heads_of(vp), preferred_element_type=F32
    ) + jnp.einsum("htcqk,ckhd->tcqhd", (p_c / total).astype(BF16), vch, preferred_element_type=F32)
    return o.reshape(q.shape).astype(BF16), top + jnp.log(total)


def attend_cont_back(q, kp, vp, kc, vc, do, lse, length):
    tops, rows, width = q.shape
    conts = rows // length
    qh = heads_of(q.reshape(tops, conts, length, width))
    gh = heads_of(do.reshape(tops, conts, length, width))
    kch = heads_of(kc.reshape(conts, length, width))
    vch = heads_of(vc.reshape(conts, length, width))
    kph, vph = heads_of(kp), heads_of(vp)
    s_p, s_c = cont_scores(qh, kph, kch, length)
    p_p, p_c = jnp.exp(s_p - lse), jnp.exp(s_c - lse)
    dp_p = jnp.einsum("tcqhd,khd->htcqk", gh, vph, preferred_element_type=F32)
    dp_c = jnp.einsum("tcqhd,ckhd->htcqk", gh, vch, preferred_element_type=F32)
    delta = jnp.sum(p_p * dp_p, axis=-1, keepdims=True) + jnp.sum(p_c * dp_c, axis=-1, keepdims=True)
    ds_p = (p_p * (dp_p - delta)).astype(BF16)
    ds_c = (p_c * (dp_c - delta)).astype(BF16)
    dq = jnp.einsum("htcqk,khd->tcqhd", ds_p, kph, preferred_element_type=F32) + jnp.einsum(
        "htcqk,ckhd->tcqhd", ds_c, kch, preferred_element_type=F32
    )
    dkp = jnp.einsum("htcqk,tcqhd->khd", ds_p, qh, preferred_element_type=F32) * HD**-0.5
    dkc = jnp.einsum("htcqk,tcqhd->ckhd", ds_c, qh, preferred_element_type=F32) * HD**-0.5
    dvp = jnp.einsum("htcqk,tcqhd->khd", p_p.astype(BF16), gh, preferred_element_type=F32)
    dvc = jnp.einsum("htcqk,tcqhd->ckhd", p_c.astype(BF16), gh, preferred_element_type=F32)
    flat = lambda m: m.reshape(-1, width)
    return (dq * HD**-0.5).reshape(q.shape).astype(BF16), flat(dkp), flat(dvp), flat(dkc), flat(dvc)


def on_device(
    prompt_in,
    cont_in,
    cotan_prompt,
    cotan_cont,
    routes_attn_p,
    routes_attn_c,
    routes_ffn_p,
    routes_ffn_c,
    adapter_pick,
    norm_gains,
    router_attn,
    router_ffn,
    w_kv,
    w_query,
    w_out,
    w_gate_up,
    w_down,
    ada_in,
    ada_out,
    ada_down,
    ada_ffn,
):
    features = prompt_in.shape[2]
    n_attn = w_query.shape[0]
    n_ffn = w_down.shape[0]
    shards = lax.axis_size("shard")
    reps = lax.axis_size("rep")
    rep_id = lax.axis_index("rep")
    cont_len = cont_in.shape[2]
    sizes = (prompt_in.shape[1], cont_in.shape[1] * cont_len)
    width = w_kv.shape[2]
    both = range(2)

    def gather(values):
        return lax.all_gather(values, "shard", axis=0, tiled=True)

    def scatter(values):
        return lax.psum_scatter(values, "shard", scatter_dimension=0, tiled=True)

    flat = lambda m: m[0].reshape(-1, m.shape[-1])
    x_own = [flat(prompt_in), flat(cont_in)]
    c_own = [flat(cotan_prompt), flat(cotan_cont)]
    ra_own = [flat(routes_attn_p), flat(routes_attn_c)]
    rf_own = [flat(routes_ffn_p), flat(routes_ffn_c)]
    chosen = adapter_pick[0]
    own_in = lax.dynamic_index_in_dim(ada_in, chosen, 0, keepdims=False)
    own_out = lax.dynamic_index_in_dim(ada_out, chosen, 0, keepdims=False)
    own_down = lax.dynamic_index_in_dim(ada_down, chosen, 0, keepdims=False)
    own_ffn = lax.dynamic_index_in_dim(ada_ffn, chosen, 0, keepdims=False)
    gain_one = norm_gains[0].astype(F32)
    gain_two = norm_gains[1].astype(F32)

    x_all = [gather(m) for m in x_own]
    routes_own = jnp.concatenate(
        [jnp.concatenate([ra_own[i], rf_own[i]], axis=1) for i in both], axis=0
    )
    routes_all = lax.all_gather(routes_own, "shard", axis=0)
    tops = ra_own[0].shape[1]
    part = [routes_all[:, : sizes[0]], routes_all[:, sizes[0] :]]
    part = [m.reshape(-1, 2 * tops) for m in part]
    ra = [m[:, :tops] for m in part]
    rf = [m[:, tops:] for m in part]
    factors = lax.all_gather(
        jnp.concatenate([own_in[:3], own_in[4:6], own_out[3:5]], axis=0), "shard", axis=2, tiled=True
    )
    a_qkv, a_ff, b_o, b_down = factors[:3], factors[3:5], factors[5], factors[6]
    b_qkv, a_o = own_out[:3], own_in[3]
    piece = width // reps
    mine = lax.dynamic_index_in_dim(
        w_out.reshape(n_attn, shards, reps, piece, w_out.shape[2]), rep_id, 2, keepdims=False
    )
    turned = lax.all_to_all(mine, "shard", 1, 3, tiled=True).reshape(n_attn, piece, features)
    w_o = lax.all_gather(turned, "rep", axis=1, tiled=True)
    c_all = [gather(m) for m in c_own]

    n1, wa, low1, q, k, v = [], [], [], [], [], []
    for i in both:
        normed, _ = norm_rows(x_all[i].astype(F32), gain_one)
        normed = normed.astype(BF16)
        n1.append(normed)
        wa.append(route_shares(dot32(normed, router_attn), ra[i]))
        low = jnp.einsum("nd,jrd->jnr", normed, a_qkv, preferred_element_type=F32)
        low1.append(low)
        shift = exact_mm(low[0], b_qkv[0].astype(F32))
        per_expert = jnp.einsum("nd,edk->enk", normed, w_query, preferred_element_type=F32) + shift
        q.append(pick_expert(per_expert, ra[i]).astype(BF16))
        k.append((dot32(normed, w_kv[0]) + exact_mm(low[1], b_qkv[1].astype(F32))).astype(BF16))
        v.append((dot32(normed, w_kv[1]) + exact_mm(low[2], b_qkv[2].astype(F32))).astype(BF16))
    o, lse = [None, None], [None, None]
    o[0], lse[0] = attend_prompt(q[0], k[0], v[0])
    o[1], lse[1] = attend_cont(q[1], k[0], v[0], k[1], v[1], cont_len)
    w_o_flat = w_o.reshape(n_attn * width, features)
    h1, n2_own, r2, o_sum, low_o = [], [], [], [], []
    for i in both:
        weighted = o[i].astype(F32) * wa[i].T[:, :, None]
        total = jnp.sum(weighted, axis=0)
        low = exact_mm(total, a_o.astype(F32).T)
        o_sum.append(total)
        low_o.append(low)
        partial = dot32(spread_expert(weighted.astype(BF16), ra[i], n_attn), w_o_flat) + exact_mm(
            low, b_o.astype(F32)
        )
        hidden = x_own[i].astype(F32) + scatter(partial.astype(BF16)).astype(F32)
        normed, inverse = norm_rows(hidden, gain_two)
        h1.append(hidden)
        r2.append(inverse)
        n2_own.append(normed.astype(BF16))

    n2 = [gather(m) for m in n2_own]
    outs, dh1 = [], []
    g_a_ff = jnp.zeros(a_ff.shape, F32)
    g_c_ff = jnp.zeros(own_ffn.shape, F32)
    g_b_down = jnp.zeros(b_down.shape, F32)
    g_a_down = jnp.zeros(own_down.shape, F32)
    for i in both:
        hot = slot_onehots(rf[i], n_ffn, sizes[i])
        wf = route_shares(dot32(n2[i], router_ffn), rf[i])
        wf_rows = jnp.sum(wf[:, :, None] * hits(rf[i], n_ffn), axis=1).reshape(shards, sizes[i], n_ffn)
        wf_slots = jnp.einsum("besr,bre->ebs", hot.astype(F32), wf_rows, precision=HIGHEST)
        blocks = lambda m: m.reshape(shards, sizes[i], m.shape[-1])
        to_slots = lambda m: jnp.einsum(
            "besr,brd->ebsd", hot, blocks(m), preferred_element_type=F32
        ).astype(BF16).reshape(n_ffn, -1, m.shape[-1])
        to_rows = lambda m: jnp.einsum(
            "besr,ebsd->brd", hot, m.reshape(n_ffn, shards, -1, m.shape[-1]), preferred_element_type=F32
        ).reshape(-1, m.shape[-1])
        xs, cs = to_slots(n2[i]), to_slots(c_all[i])
        wf_slots = wf_slots.reshape(n_ffn, -1)
        y_parts, d_parts, dw_parts = [], [], []
        for e in range(n_ffn):
            low = [dot32(xs[e], a_ff[j].T) for j in both]
            g = [dot32(xs[e], w_gate_up[e, j]) + exact_mm(low[j], own_ffn[j].astype(F32)) for j in both]
            sig = jax.nn.sigmoid(g[0])
            act = (g[0] * sig * g[1]).astype(BF16)
            low_down = dot32(act, own_down.T)
            y = dot32(act, w_down[e]) + exact_mm(low_down, b_down.astype(F32))
            ws = wf_slots[e][:, None]
            c_low = dot32(cs[e], b_down.T)
            d_act = dot32(cs[e], w_down[e].T) + exact_mm(c_low, own_down.astype(F32))
            dw_parts.append(jnp.sum(d_act * act.astype(F32), axis=-1, keepdims=True))
            d_act = d_act * ws
            dg = [
                (d_act * g[1] * sig * (1.0 + g[0] * (1.0 - sig))).astype(BF16),
                (d_act * g[0] * sig).astype(BF16),
            ]
            d_low = [dot32(dg[j], own_ffn[j].T) for j in both]
            dx = sum(
                dot32(dg[j], w_gate_up[e, j].T) + exact_mm(d_low[j], a_ff[j].astype(F32)) for j in both
            )
            y_parts.append((ws * y).astype(BF16))
            d_parts.append(dx.astype(BF16))
            g_b_down = g_b_down + dot32((ws * low_down).astype(BF16).T, cs[e])
            g_a_down = g_a_down + dot32((ws * c_low).astype(BF16).T, act)
            g_c_ff = g_c_ff + jnp.stack([dot32(low[j].astype(BF16).T, dg[j]) for j in both])
            g_a_ff = g_a_ff + jnp.stack([dot32(d_low[j].astype(BF16).T, xs[e]) for j in both])
        y_rows = scatter(to_rows(jnp.stack(y_parts)).astype(BF16)).astype(F32)
        outs.append((h1[i] + y_rows).astype(BF16))
        d_rows = scatter(to_rows(jnp.stack(d_parts)).astype(BF16)).astype(F32)
        dw = jnp.stack(dw_parts).reshape(n_ffn, shards, -1)
        dw_rows = jnp.einsum("besr,ebs->bre", hot.astype(F32), dw, precision=HIGHEST)
        dw_rows = scatter(dw_rows.reshape(-1, n_ffn))
        wf_own = route_shares(dot32(n2_own[i], router_ffn), rf_own[i])
        dw_top = jnp.einsum("rte,re->rt", hits(rf_own[i], n_ffn), dw_rows, precision=HIGHEST)
        d_logits = shares_back(wf_own, rf_own[i], n_ffn, dw_top)
        d_rows = d_rows + exact_mm(d_logits, router_ffn.astype(F32).T)
        dh1.append(c_own[i].astype(F32) + norm_back(h1[i], r2[i], gain_two, d_rows))

    dh1_all = [gather(m.astype(BF16)) for m in dh1]
    g_a_o = jnp.zeros(a_o.shape, F32)
    g_b_o = jnp.zeros(b_o.shape, F32)
    do, dwa = [], []
    for i in both:
        d_low = dot32(dh1_all[i], b_o.T)
        per_expert = jnp.einsum("nd,ekd->enk", dh1_all[i], w_o, preferred_element_type=F32)
        per_expert = per_expert + exact_mm(d_low, a_o.astype(F32))
        picked = pick_expert(per_expert, ra[i])
        dwa.append(jnp.sum(picked * o[i].astype(F32), axis=-1).T)
        do.append((picked * wa[i].T[:, :, None]).astype(BF16))
        g_a_o = g_a_o + dot32(d_low.astype(BF16).T, o_sum[i].astype(BF16))
        g_b_o = g_b_o + dot32(low_o[i].astype(BF16).T, dh1_all[i])
    dq, dk, dv = [None, None], [None, None], [None, None]
    dq[0], dk[0], dv[0] = attend_prompt_back(q[0], k[0], v[0], do[0], lse[0])
    dq[1], dkp, dvp, dk[1], dv[1] = attend_cont_back(
        q[1], k[0], v[0], k[1], v[1], do[1], lse[1], cont_len
    )
    dk[0], dv[0] = dk[0] + dkp, dv[0] + dvp
    g_a_qkv = jnp.zeros(a_qkv.shape, F32)
    g_b_qkv = jnp.zeros(b_qkv.shape, F32)
    grads = []
    for i in both:
        dq_sum = jnp.sum(dq[i].astype(F32), axis=0).astype(BF16)
        dkv = [dk[i].astype(BF16), dv[i].astype(BF16)]
        d_mats = [dq_sum] + dkv
        d_low = [dot32(d_mats[j], b_qkv[j].T) for j in range(3)]
        d_rows = jnp.einsum(
            "nek,edk->nd",
            spread_expert(dq[i], ra[i], n_attn).reshape(-1, n_attn, width),
            w_query,
            preferred_element_type=F32,
        )
        d_rows = d_rows + dot32(dkv[0], w_kv[0].T) + dot32(dkv[1], w_kv[1].T)
        d_rows = d_rows + sum(exact_mm(d_low[j], a_qkv[j].astype(F32)) for j in range(3))
        g_a_qkv = g_a_qkv + jnp.stack([dot32(d_low[j].astype(BF16).T, n1[i]) for j in range(3)])
        g_b_qkv = g_b_qkv + jnp.stack(
            [dot32(low1[i][j].astype(BF16).T, d_mats[j]) for j in range(3)]
        )
        d_rows = scatter(d_rows.astype(BF16)).astype(F32)
        dw_top = scatter(dwa[i])
        x32 = x_own[i].astype(F32)
        normed, inverse = norm_rows(x32, gain_one)
        wa_own = route_shares(dot32(normed.astype(BF16), router_attn), ra_own[i])
        d_logits = shares_back(wa_own, ra_own[i], n_attn, dw_top)
        d_rows = d_rows + exact_mm(d_logits, router_attn.astype(F32).T)
        grads.append(dh1[i] + norm_back(x32, inverse, gain_one, d_rows))

    parts = jnp.concatenate([g_a_qkv, g_a_ff, g_b_o[None], g_b_down[None]], axis=0)
    parts = lax.psum_scatter(parts.astype(BF16), "shard", scatter_dimension=2, tiled=True).astype(F32)
    g_in = jnp.concatenate([parts[:3], g_a_o[None], parts[3:5]], axis=0)
    g_out = jnp.concatenate([g_b_qkv, parts[5:7]], axis=0)
    slot_hot = (jnp.arange(ada_in.shape[0], dtype=jnp.int32) == chosen).astype(F32)

    def over_groups(grad):
        spread = slot_hot.reshape((-1,) + (1,) * grad.ndim) * grad[None]
        return lax.psum(spread.astype(BF16), "rep").astype(F32)

    shape_c = (1,) + cont_in.shape[1:]
    return (
        outs[0][None],
        outs[1].reshape(shape_c),
        grads[0][None],
        grads[1].reshape(shape_c),
        over_groups(g_in),
        over_groups(g_out),
        over_groups(g_a_down),
        over_groups(g_c_ff),
    )


def solution(mesh):
    rows = (P("rep", "shard", None), P("rep", "shard", None, None))
    last = (
        P(None, None, None, "shard"),
        P(None, None, None, "shard"),
        P(None, None, "shard"),
        P(None, None, None, "shard"),
    )
    in_specs = (
        rows * 4
        + (P("rep"), P(), P(), P())
        + (P(None, None, "shard"),) * 3
        + (P(None, None, None, "shard"), P(None, "shard", None))
        + last
    )
    return jax.shard_map(
        on_device, mesh=mesh, in_specs=in_specs, out_specs=rows * 2 + last, check_vma=False
    )
```

```python
import functools

import jax
import jax.numpy as jnp
from jax import lax
from jax.experimental import pallas as pl
from jax.experimental.pallas import tpu as pltpu
from jax.sharding import PartitionSpec as P

HD = 128
SCALE = HD**-0.5
EPSILON = 1e-05
HIGHEST = lax.Precision.HIGHEST
F32 = jnp.float32
BF16 = jnp.bfloat16
EXT = 128


def dot32(former, latter):
    return jnp.dot(former, latter, preferred_element_type=F32)


def dot_nt(former, latter):
    return lax.dot_general(former, latter, (((1,), (1,)), ((), ())), preferred_element_type=F32)


def dot_tn(former, latter):
    return lax.dot_general(former, latter, (((0,), (0,)), ((), ())), preferred_element_type=F32)


def exact_mm(former, latter):
    return jnp.dot(former, latter, precision=HIGHEST)


def split_low(values):
    high = values.astype(BF16)
    return [high, (values - high.astype(F32)).astype(BF16)]


def twice(values):
    return jnp.concatenate([values, values], axis=0)


def norm_rows(values, scaling):
    inverse = lax.rsqrt(jnp.mean(values * values, axis=-1, keepdims=True) + EPSILON)
    return (values * inverse * scaling, inverse)


def norm_back(values, inverse, scaling, upstream):
    weighted = upstream * scaling
    inner_mean = jnp.mean(weighted * values, axis=-1, keepdims=True)
    return inverse * weighted - values * (inverse * inverse * inverse) * inner_mean


def capacity(block_rows, experts, top_count):
    return min(block_rows, ((block_rows * top_count + experts - 1) // experts + 7) // 8 * 8 + 8)


def hits(routes, experts):
    labels = jnp.arange(experts, dtype=jnp.int32)
    return (routes[:, :, None] == labels[None, None, :]).astype(F32)


def slot_onehots(routes, experts, block):
    rows, top_count = routes.shape
    slot_cap = capacity(block, experts, top_count)
    member = jnp.sum(hits(routes, experts), axis=1).reshape(-1, 2, block, experts)
    place = jnp.arange(block, dtype=jnp.int32)
    before = (place[None, :] < place[:, None]).astype(BF16)
    ranked = jnp.einsum("rq,phqe->phre", before, member.astype(BF16), preferred_element_type=F32)
    ranked = ranked + jnp.arange(2, dtype=F32)[None, :, None, None] * slot_cap
    slot_of = jnp.where(member > 0, ranked, -1.0).reshape(-1, 2 * block, experts)
    slots = jnp.arange(2 * slot_cap, dtype=F32)
    return (slot_of.transpose(2, 0, 1)[:, :, None, :] == slots[None, None, :, None]).astype(BF16)


def route_shares(logits, routes):
    chosen = jnp.einsum("rte,re->rt", hits(routes, logits.shape[1]), logits, precision=HIGHEST)
    return jax.nn.softmax(chosen, axis=-1)


def shares_back(shares, routes, experts, d_shares):
    d_chosen = shares * (d_shares - jnp.sum(shares * d_shares, axis=-1, keepdims=True))
    return jnp.sum(d_chosen[:, :, None] * hits(routes, experts), axis=1)


def with_ext(rows, columns):
    used = sum(c.shape[1] for c in columns)
    columns = [c.astype(BF16) for c in columns]
    blank = jnp.zeros((rows.shape[0], EXT - used), BF16)
    return jnp.concatenate([rows.astype(BF16)] + columns + [blank], axis=1)


def whole(*shape):
    return pl.BlockSpec(
        shape, lambda *ids: (0,) * len(shape), pipeline_mode=pl.Buffered(buffer_count=1)
    )


def anywhere():
    return pl.BlockSpec(memory_space=pl.ANY)


def kernel_params(dims, mib):
    return pltpu.CompilerParams(
        dimension_semantics=("arbitrary",) * dims, vmem_limit_bytes=mib * 2**20
    )


def pair_rows(ref, span):
    start, rows = span
    return ref[:, start : start + rows, :].reshape(2 * rows, ref.shape[2])


def ext_choice(ext, tops, experts, rank):
    ext = ext[...].astype(F32)
    at = 3 * rank
    shares = [ext[:, at + t : at + t + 1] + ext[:, at + tops + t : at + tops + t + 1] for t in range(tops)]
    at = at + 2 * tops
    chosen = [[ext[:, at + t : at + t + 1] == e for e in range(experts)] for t in range(tops)]
    return shares, chosen


def qkv_kernel(span, tops, rank, load, routes, w_q, w_kv, fac_a, fac_b, q, k, v, low_out):
    features = w_q.shape[1]
    experts = w_q.shape[0]
    rows = span[1]
    block = pair_rows(load, span)
    n1 = block
    route = pair_rows(routes, span)[:, :tops].astype(F32)
    chosen = [[route[:, t : t + 1] == e for e in range(experts)] for t in range(tops)]
    low = dot_nt(n1, fac_a[...])
    logits = [
        sum(jnp.where(chosen[t][e], low[:, 3 * rank + e : 3 * rank + e + 1], 0.0) for e in range(experts))
        for t in range(tops)
    ]
    peak = functools.reduce(jnp.maximum, logits)
    shares = [jnp.exp(m - peak) for m in logits]
    total = sum(shares)
    shares = split_low(jnp.concatenate([m / total for m in shares], axis=1))
    low_out[...] = jnp.concatenate(
        [low[:, : 3 * rank].astype(BF16)]
        + shares
        + [route.astype(BF16), jnp.zeros((2 * rows, EXT - 3 * rank - 3 * tops), BF16)],
        axis=1,
    )
    shift = []
    for j in range(3):
        wide = jnp.concatenate(split_low(low[:, rank * j : rank * (j + 1)]), axis=1)
        shift.append(dot32(wide, twice(fac_b[j])))
    k[...] = (dot32(n1, w_kv[0]) + shift[1]).astype(BF16)
    v[...] = (dot32(n1, w_kv[1]) + shift[2]).astype(BF16)
    picked = [shift[0]] * tops
    for e in range(experts):
        here = dot32(n1, w_q[e])
        for t in range(tops):
            picked[t] = picked[t] + jnp.where(chosen[t][e], here, 0.0)
    for t in range(tops):
        q[t] = picked[t].astype(BF16)


def qkv_call(load, routes, span, tops, w_q, w_kv, fac_a, fac_b):
    shards, held, wide = load.shape
    rows = span[1]
    width = w_q.shape[2]
    total = shards * rows
    rank = fac_b.shape[1]
    out = lambda n: pl.BlockSpec((2 * rows, n), lambda p: (p, 0))
    return pl.pallas_call(
        functools.partial(qkv_kernel, span, tops, rank),
        grid=(shards // 2,),
        in_specs=[
            pl.BlockSpec((2, held, wide), lambda p: (p, 0, 0)),
            pl.BlockSpec((2,) + routes.shape[1:], lambda p: (p, 0, 0)),
            whole(*w_q.shape),
            whole(*w_kv.shape),
            whole(*fac_a.shape),
            whole(*fac_b.shape),
        ],
        out_specs=[
            pl.BlockSpec((tops, 2 * rows, width), lambda p: (0, p, 0)),
            out(width),
            out(width),
            out(EXT),
        ],
        out_shape=[
            jax.ShapeDtypeStruct((tops, total, width), BF16),
            jax.ShapeDtypeStruct((total, width), BF16),
            jax.ShapeDtypeStruct((total, width), BF16),
            jax.ShapeDtypeStruct((total, EXT), BF16),
        ],
        compiler_params=kernel_params(1, 56),
        cost_estimate=pl.CostEstimate(
            flops=2 * total * w_q.shape[1] * width * (w_q.shape[0] + 2),
            bytes_accessed=2 * (w_q.size + w_kv.size + load.size),
            transcendentals=0,
        ),
        name="qkv",
    )(load, routes, w_q, w_kv, fac_a, fac_b)


def out_kernel(tops, ext, o, w_o, fac_a, fac_b, out):
    experts = w_o.shape[0]
    shares, chosen = ext_choice(ext, tops, experts, fac_a.shape[0])
    parts = [o[t].astype(F32) * shares[t] for t in range(tops)]
    low = dot_nt(sum(parts).astype(BF16), fac_a[...])
    total = dot32(jnp.concatenate(split_low(low), axis=1), twice(fac_b[...]))
    for e in range(experts):
        here = sum(jnp.where(chosen[t][e], parts[t], 0.0) for t in range(tops)).astype(BF16)
        total = total + dot32(here, w_o[e])
    out[...] = total.astype(BF16)


def out_call(ext, rows, o, w_o, fac_a, fac_b):
    tops, total, width = o.shape
    features = w_o.shape[2]
    return pl.pallas_call(
        functools.partial(out_kernel, tops),
        grid=(total // (2 * rows),),
        in_specs=[
            pl.BlockSpec((2 * rows, EXT), lambda p: (p, 0)),
            pl.BlockSpec((tops, 2 * rows, width), lambda p: (0, p, 0)),
            whole(*w_o.shape),
            whole(*fac_a.shape),
            whole(*fac_b.shape),
        ],
        out_specs=pl.BlockSpec((2 * rows, features), lambda p: (p, 0)),
        out_shape=jax.ShapeDtypeStruct((total, features), BF16),
        compiler_params=kernel_params(1, 56),
        cost_estimate=pl.CostEstimate(
            flops=2 * total * w_o.size,
            bytes_accessed=2 * (w_o.size + o.size + total * features),
            transcendentals=0,
        ),
        name="project_out",
    )(ext, o, w_o, fac_a, fac_b)


def out_back_kernel(tops, ext, dh, o, w_o, fac_a, fac_b, do, dw, grad_a, grad_b):
    experts = w_o.shape[0]
    shares, chosen = ext_choice(ext, tops, experts, fac_a.shape[0])
    block = dh[...].reshape(-1, dh.shape[2])
    rows = block.shape[0]
    low = split_low(dot_nt(block, fac_b[...]))
    shift = dot32(jnp.concatenate(low, axis=1), twice(fac_a[...]))
    picked = [shift] * tops
    for e in range(experts):
        here = dot_nt(block, w_o[e])
        for t in range(tops):
            picked[t] = picked[t] + jnp.where(chosen[t][e], here, 0.0)
    lane = lax.broadcasted_iota(jnp.int32, (rows, EXT), 1)
    back = jnp.zeros((rows, EXT), F32)
    total = None
    for t in range(tops):
        value = o[t].astype(F32)
        back = back + jnp.where(lane == t, jnp.sum(picked[t] * value, axis=1, keepdims=True), 0.0)
        do[t] = (picked[t] * shares[t]).astype(BF16)
        value = value * shares[t]
        total = value if total is None else total + value
    dw[...] = back.astype(BF16)
    total = total.astype(BF16)

    @pl.when(pl.program_id(0) == 0)
    def _():
        grad_a[...] = jnp.zeros_like(grad_a)
        grad_b[...] = jnp.zeros_like(grad_b)

    grad_a[...] += dot_tn(low[0], total)
    grad_b[...] += dot_tn(dot_nt(total, fac_a[...]).astype(BF16), block)


def out_back_call(ext, rows, dh, o, w_o, fac_a, fac_b):
    tops, total, width = o.shape
    rank, features = fac_b.shape
    two = pl.BlockSpec((tops, 2 * rows, width), lambda p: (0, p, 0))
    row = pl.BlockSpec((2 * rows, EXT), lambda p: (p, 0))
    return pl.pallas_call(
        functools.partial(out_back_kernel, tops),
        grid=(total // (2 * rows),),
        in_specs=[
            row,
            pl.BlockSpec((2,) + dh.shape[1:], lambda p: (p, 0, 0)),
            two,
            whole(*w_o.shape),
            whole(*fac_a.shape),
            whole(*fac_b.shape),
        ],
        out_specs=[
            two,
            row,
            pl.BlockSpec((rank, width), lambda p: (0, 0)),
            pl.BlockSpec((rank, features), lambda p: (0, 0)),
        ],
        out_shape=[
            jax.ShapeDtypeStruct(o.shape, BF16),
            jax.ShapeDtypeStruct((total, EXT), BF16),
            jax.ShapeDtypeStruct((rank, width), F32),
            jax.ShapeDtypeStruct((rank, features), F32),
        ],
        compiler_params=kernel_params(1, 56),
        cost_estimate=pl.CostEstimate(
            flops=2 * total * w_o.size,
            bytes_accessed=2 * (w_o.size + 2 * o.size + total * features),
            transcendentals=0,
        ),
        name="project_out_back",
    )(ext, dh, o, w_o, fac_a, fac_b)


def qkv_back_kernel(span, tops, rank, load, dq, dk, dv, dw, low_in, w_q, w_kv, fac_b, out, grad_a, grad_b):
    experts, features, _ = w_q.shape
    rows = span[1]
    block = pair_rows(load, span)
    _, chosen = ext_choice(low_in, tops, experts, rank)
    total = dot_nt(dk[...], w_kv[0]) + dot_nt(dv[...], w_kv[1])
    blank = jnp.zeros(dk.shape, BF16)
    for e in range(experts):
        here = blank
        for t in range(tops):
            here = jnp.where(chosen[t][e], dq[t], here)
        total = total + dot_nt(here, w_q[e])
    dq_sum = sum(dq[t].astype(F32) for t in range(tops)).astype(BF16)
    sides = [dq_sum, dk[...], dv[...]]
    low = jnp.concatenate([dot_nt(sides[j], fac_b[j]) for j in range(3)], axis=1)
    out[:, :features] = total.astype(BF16)
    out[:, features:] = jnp.concatenate(
        [dw[:, :rank], low.astype(BF16), jnp.zeros((2 * rows, EXT - 4 * rank), BF16)], axis=1
    )

    @pl.when(pl.program_id(0) == 0)
    def _():
        grad_a[...] = jnp.zeros_like(grad_a)
        grad_b[...] = jnp.zeros_like(grad_b)

    grad_a[...] += dot_tn(low.astype(BF16), block)
    for j in range(3):
        grad_b[j] += dot_tn(low_in[:, rank * j : rank * (j + 1)], sides[j])


def qkv_back_call(load, span, dq, dk, dv, dw, low_in, w_q, w_kv, fac_b, earlier):
    tops, total, width = dq.shape
    rows = span[1]
    features = w_q.shape[1]
    rank = fac_b.shape[1]
    row = lambda n: pl.BlockSpec((2 * rows, n), lambda p: (p, 0))

    def kernel(*refs):
        qkv_back_kernel(span, tops, rank, *refs[:9], *refs[9 + len(earlier) :])

    return pl.pallas_call(
        kernel,
        grid=(total // (2 * rows),),
        in_specs=[
            pl.BlockSpec((2,) + load.shape[1:], lambda p: (p, 0, 0)),
            pl.BlockSpec((tops, 2 * rows, width), lambda p: (0, p, 0)),
            row(width),
            row(width),
            row(EXT),
            row(EXT),
            whole(*w_q.shape),
            whole(*w_kv.shape),
            whole(*fac_b.shape),
        ]
        + [anywhere() for _ in earlier],
        out_specs=[
            row(features + EXT),
            pl.BlockSpec((3 * rank, features), lambda p: (0, 0)),
            pl.BlockSpec((3, rank, width), lambda p: (0, 0, 0)),
        ],
        out_shape=[
            jax.ShapeDtypeStruct((total, features + EXT), BF16),
            jax.ShapeDtypeStruct((3 * rank, features), F32),
            jax.ShapeDtypeStruct((3, rank, width), F32),
        ],
        compiler_params=kernel_params(1, 56),
        cost_estimate=pl.CostEstimate(
            flops=2 * total * (w_q.size + w_kv.size),
            bytes_accessed=2 * (w_q.size + w_kv.size + 2 * load.size),
            transcendentals=0,
        ),
        name="qkv_back",
    )(load, dq, dk, dv, dw, low_in, w_q, w_kv, fac_b, *earlier)


def ffn_tiles(units):
    if units % 128:
        return [(0, units)]
    return [(start, min(512, units - start)) for start in range(0, units, 512)]


def ffn_kernel(tiles, rank, begin, hot, n2, c, w_gu, w_d, fac_gu, fac_d, y_out, dx_out, g_out, xs, cs, acc_y, acc_d, buf_gu, buf_d, sems):
    e = pl.program_id(0)
    here = pl.num_programs(0)
    experts, _, features = w_d.shape
    count = len(tiles)
    pairs, slots, _ = hot.shape[1:]
    rows = n2.shape[1]
    total = pairs * slots
    side = pl.ds(features, EXT)

    def copies(expert, t, slot):
        start, size = tiles[t]
        cols = pl.ds(start, size)
        got = pl.ds(0, size)
        pairs_of = [
            (w_gu.at[begin + expert, 0, :, cols], buf_gu.at[slot, 0, pl.ds(0, features), got]),
            (w_gu.at[begin + expert, 1, :, cols], buf_gu.at[slot, 1, pl.ds(0, features), got]),
            (w_d.at[begin + expert, cols, :], buf_d.at[slot, got, pl.ds(0, features)]),
            (fac_gu.at[:, :, cols], buf_gu.at[slot, :, side, got]),
            (fac_d.at[cols, :], buf_d.at[slot, got, side]),
        ]
        return [pltpu.make_async_copy(*m, sems.at[slot, n]) for n, m in enumerate(pairs_of)]

    @pl.when(e == 0)
    def _():
        for m in copies(0, 0, 0):
            m.start()
        g_out[...] = jnp.zeros_like(g_out)

    for p in range(pairs):
        spot = pl.ds(p * slots, slots)
        xs[spot, :] = dot32(hot[0, p], n2[2 * p : 2 * p + 2].reshape(2 * rows, -1)).astype(BF16)
        cs[spot, :] = dot32(hot[0, p], c[2 * p : 2 * p + 2].reshape(2 * rows, -1)).astype(BF16)
    lane = lax.broadcasted_iota(jnp.int32, (total, EXT), 1)
    ext = xs[:, features:]
    mine = (lane == 4 * rank + begin + e) | (lane == 4 * rank + experts + begin + e)
    share = jnp.sum(jnp.where(mine, ext.astype(F32), 0.0), axis=1, keepdims=True)
    low = [ext[:, :rank], ext[:, 2 * rank : 3 * rank], cs[:, features : features + rank]]
    low[2] = (low[2].astype(F32) * share).astype(BF16)
    dw = None
    for t, (start, size) in enumerate(tiles):
        slot = lax.rem(e * count + t, 2)
        for m in copies(e, t, slot):
            m.wait()
        if t + 1 < count:
            for m in copies(e, t + 1, 1 - slot):
                m.start()
        else:

            @pl.when(e + 1 < here)
            def _():
                for m in copies(e + 1, 0, 1 - slot):
                    m.start()

        spot = pl.ds(0, size)
        cols = pl.ds(start, size)
        wg, wu, wd = buf_gu.at[slot, 0, :, spot], buf_gu.at[slot, 1, :, spot], buf_d.at[slot, spot, :]
        g0 = dot32(xs[...], wg[...])
        g1 = dot32(xs[...], wu[...])
        da = dot_nt(cs[...], wd[...])
        sig = 1.0 / (1.0 + jnp.exp(-g0))
        silu = g0 * sig
        act = (silu * g1).astype(BF16)
        now = jnp.sum(da * act.astype(F32), axis=1, keepdims=True)
        dw = now if dw is None else dw + now
        da = da * share
        dg0 = (da * g1 * (sig + silu * (1.0 - sig))).astype(BF16)
        dg1 = (da * silu).astype(BF16)
        g_out[0, :, cols] += dot_tn(low[0], dg0)
        g_out[1, :, cols] += dot_tn(low[1], dg1)
        g_out[2, :, cols] += dot_tn(low[2], act)
        if t == 0 and count > 1:
            acc_y[...] = dot32(act, wd[...])
            acc_d[...] = dot_nt(dg0, wg[...]) + dot_nt(dg1, wu[...])
        elif t + 1 < count:
            acc_y[...] += dot32(act, wd[...])
            acc_d[...] += dot_nt(dg0, wg[...]) + dot_nt(dg1, wu[...])
        else:
            y = dot32(act, wd[...])
            d = dot_nt(dg0, wg[...]) + dot_nt(dg1, wu[...])
            if count > 1:
                y, d = y + acc_y[...], d + acc_d[...]
            y_out[0] = (y * share).astype(BF16)
            dx_out[0] = d.astype(BF16)
            d = jnp.where(lane == 4 * rank + begin + e, dw, d[:, features:])
            dx_out[0, :, features:] = d.astype(BF16)


def ffn_call(hot, n2, c, w_gu, w_d, fac_gu, fac_d, rank, earlier, begin, experts):
    _, pairs, slots, _ = hot.shape
    total = pairs * slots
    units, features = w_d.shape[1:]
    wide = features + EXT
    tiles = ffn_tiles(units)
    widest = max(size for _, size in tiles)
    one = lambda *s: pl.BlockSpec((1,) + s, lambda e: (e,) + (0,) * len(s))

    def kernel(*refs):
        ffn_kernel(tiles, rank, begin, *refs[:7], *refs[8:])

    return pl.pallas_call(
        kernel,
        grid=(experts,),
        in_specs=[
            pl.BlockSpec((1,) + hot.shape[1:], lambda e: (begin + e, 0, 0, 0)),
            whole(*n2.shape),
            whole(*c.shape),
        ]
        + [anywhere() for _ in range(5)],
        out_specs=[
            one(total, wide),
            one(total, wide),
            pl.BlockSpec((3, rank, units), lambda e: (0, 0, 0)),
        ],
        out_shape=[
            jax.ShapeDtypeStruct((experts, total, wide), BF16),
            jax.ShapeDtypeStruct((experts, total, wide), BF16),
            jax.ShapeDtypeStruct((3, rank, units), F32),
        ],
        scratch_shapes=[
            pltpu.VMEM((total, wide), BF16),
            pltpu.VMEM((total, wide), BF16),
            pltpu.VMEM((total, wide), F32),
            pltpu.VMEM((total, wide), F32),
            pltpu.VMEM((2, 2, wide, widest), BF16),
            pltpu.VMEM((2, widest, wide), BF16),
            pltpu.SemaphoreType.DMA((2, 5)),
        ],
        compiler_params=kernel_params(1, 62),
        cost_estimate=pl.CostEstimate(
            flops=12 * experts * total * features * units,
            bytes_accessed=6 * experts * features * units + 8 * experts * total * features,
            transcendentals=experts * total * units,
        ),
        name="ffn",
    )(hot, n2, c, w_gu, w_d, fac_gu, fac_d, earlier)


def rows_call(hot, parts, source, fac, lows, keep, earlier):
    experts, pairs, slots, rows = hot.shape
    count, _, wide = parts[0].shape
    rank = fac.shape[0] // len(lows)
    features = wide - EXT
    parts = [m.reshape(count, pairs, slots, wide) for m in parts]
    by_pair = lambda n, *s: pl.BlockSpec((n, 1) + s, lambda p: (0, p, 0, 0))

    def kernel(hot, *refs):
        values, source, fac, _, out, grad = refs[: len(parts)], *refs[len(parts) :]
        total = None
        for e in range(experts):
            here = dot_tn(hot[e, 0], values[e // count][e % count, 0])
            total = here if total is None else total + here
        low = [total[:, features + at : features + at + rank] for at in lows]
        low = split_low(jnp.concatenate(low, axis=1))
        main = total[:, :features] + dot32(jnp.concatenate(low, axis=1), twice(fac[...]))
        out[:, :features] = main.astype(BF16)
        if keep:
            out[:, features:] = total[:, features:].astype(BF16)

        @pl.when(pl.program_id(0) == 0)
        def _():
            grad[...] = jnp.zeros_like(grad)

        grad[...] += dot_tn(low[0], source[:, :, :features].reshape(rows, features))

    out_wide = wide if keep else features
    return pl.pallas_call(
        kernel,
        grid=(pairs,),
        in_specs=[by_pair(experts, slots, rows)]
        + [by_pair(count, slots, wide) for _ in parts]
        + [
            pl.BlockSpec((2,) + source.shape[1:], lambda p: (p, 0, 0)),
            whole(*fac.shape),
            anywhere(),
        ],
        out_specs=[
            pl.BlockSpec((rows, out_wide), lambda p: (p, 0)),
            pl.BlockSpec(fac.shape, lambda p: (0, 0)),
        ],
        out_shape=[
            jax.ShapeDtypeStruct((pairs * rows, out_wide), BF16),
            jax.ShapeDtypeStruct(fac.shape, F32),
        ],
        compiler_params=kernel_params(1, 56),
        cost_estimate=pl.CostEstimate(
            flops=2 * hot.size * wide,
            bytes_accessed=2 * (hot.size + experts * pairs * slots * wide),
            transcendentals=0,
        ),
        name="slots_to_rows",
    )(hot, *parts, source, fac, earlier)


def whole_rows(q):
    return q.reshape(q.shape[0]*q.shape[1], q.shape[2])

def masked_pair(q, keys, diag_keys, seen):
    far = None if keys is None else dot_nt(q, keys)
    near = jnp.where(seen, dot_nt(q, diag_keys), -1e30)
    return far, near

def soft_pair(far, near):
    top = jnp.max(near, axis=1, keepdims=True)
    if far is not None: top = jnp.maximum(top, jnp.max(far, axis=1, keepdims=True))
    p_near = jnp.exp((near - top) * SCALE)
    total = jnp.sum(p_near, axis=1, keepdims=True)
    p_far = None
    if far is not None:
        p_far = jnp.exp((far - top) * SCALE)
        total = total + jnp.sum(p_far, axis=1, keepdims=True)
    return p_far, p_near, top * SCALE + jnp.log(total), 1.0 / total

def prompt_seen(tops, size):
    r = lax.broadcasted_iota(jnp.int32, (tops, size, size), 1).reshape(tops*size, size)
    k = lax.broadcasted_iota(jnp.int32, (tops*size, size), 1)
    return k <= r

def cont_seen(tops, size, length):
    r = lax.broadcasted_iota(jnp.int32, (tops, size, size), 1).reshape(tops*size, size)
    k = lax.broadcasted_iota(jnp.int32, (tops*size, size), 1)
    own = k <= r
    for start in range(length, size, length):
        own = own & ((r < start) | (k >= start))
    return own

def forward_tile(q, far_k, far_v, near_k, near_v, seen):
    far, near = masked_pair(q, far_k, near_k, seen)
    p_far, p_near, lse, inv = soft_pair(far, near)
    o = dot32(p_near.astype(BF16), near_v)
    if far is not None: o = o + dot32(p_far.astype(BF16), far_v)
    return (o * inv).astype(BF16), lse

def prompt_fwd(tile, q, k, v, o, lse):
    tops, rows, _ = q.shape
    for start in range(0, rows, tile):
        here = pl.ds(start, tile)
        out, stat = forward_tile(whole_rows(q[:, here, :]), k[:start, :] if start else None, v[:start, :] if start else None, k[here, :], v[here, :], prompt_seen(tops, tile))
        o[:, here, :] = out.reshape(tops, tile, HD)
        lse[0, :, here, :] = stat.reshape(tops, tile, 1)

def cont_fwd(length, q, kp, vp, k, v, earlier, o, lse):
    tops, size, _ = q.shape
    out, stat = forward_tile(whole_rows(q[...]), kp[...], vp[...], k[...], v[...], cont_seen(tops, size, length))
    o[...] = out.reshape(tops, size, HD)
    lse[0] = stat.reshape(tops, size, 1)

def backward_tile(q, do, lse, far_k, far_v, near_k, near_v, seen):
    far, near = masked_pair(q, far_k, near_k, seen)
    p_near = jnp.exp(near * SCALE - lse)
    dp_near = dot_nt(do, near_v)
    delta = jnp.sum(p_near * dp_near, axis=1, keepdims=True)
    if far is not None:
        p_far = jnp.exp(far * SCALE - lse)
        dp_far = dot_nt(do, far_v)
        delta = delta + jnp.sum(p_far * dp_far, axis=1, keepdims=True)
    ds_near = (p_near * (dp_near - delta)).astype(BF16)
    dq = dot32(ds_near, near_k)
    near_grads = dot_tn(ds_near, q) * SCALE, dot_tn(p_near.astype(BF16), do)
    far_grads = None
    if far is not None:
        ds_far = (p_far * (dp_far - delta)).astype(BF16)
        dq = dq + dot32(ds_far, far_k)
        far_grads = dot_tn(ds_far, q) * SCALE, dot_tn(p_far.astype(BF16), do)
    return (dq * SCALE).astype(BF16), far_grads, near_grads

def prompt_bwd(tile, q, k, v, do, lse, dq, dk, dv):
    tops, rows, _ = q.shape
    for start in range(0, rows, tile):
        here = pl.ds(start, tile)
        out, far, near = backward_tile(whole_rows(q[:, here, :]), whole_rows(do[:, here, :]), lse[0, :, here, :].reshape(tops*tile, 1),
            k[:start, :] if start else None, v[:start, :] if start else None, k[here, :], v[here, :], prompt_seen(tops, tile))
        dq[:, here, :] = out.reshape(tops, tile, HD)
        dk[here, :], dv[here, :] = near
        if start:
            dk[:start, :] += far[0]
            dv[:start, :] += far[1]

def cont_bwd(length, q, kp, vp, k, v, do, lse, dkp_in, dvp_in, dq, dkp, dvp, dk, dv, acc_k, acc_v):
    tops, size, _ = q.shape
    step = pl.program_id(1)
    @pl.when(step == 0)
    def _():
        acc_k[...] = dkp_in[...]
        acc_v[...] = dvp_in[...]
    out, far, near = backward_tile(whole_rows(q[...]), whole_rows(do[...]), lse[0].reshape(tops*size, 1), kp[...], vp[...], k[...], v[...], cont_seen(tops, size, length))
    dq[...] = out.reshape(tops, size, HD)
    dk[...], dv[...] = near[0].astype(BF16), near[1].astype(BF16)
    acc_k[...] += far[0]
    acc_v[...] += far[1]
    @pl.when(step == pl.num_programs(1) - 1)
    def _():
        dkp[...] = acc_k[...].astype(BF16)
        dvp[...] = acc_v[...].astype(BF16)

def cost(tops, rows, keys, width, products):
    return pl.CostEstimate(flops=4*tops*rows*keys*width*products, bytes_accessed=8*rows*width*tops, transcendentals=tops*rows*keys*width//HD)

def prompt_specs(tops, rows):
    by_head = pl.BlockSpec((rows, HD), lambda h: (0, h))
    two = pl.BlockSpec((tops, rows, HD), lambda h: (0, 0, h))
    stat = pl.BlockSpec((1, tops, rows, 1), lambda h: (h, 0, 0, 0))
    return by_head, two, stat

def cont_specs(tops, prompt, size):
    keys = pl.BlockSpec((prompt, HD), lambda h, i: (0, h))
    own = pl.BlockSpec((size, HD), lambda h, i: (i, h))
    two = pl.BlockSpec((tops, size, HD), lambda h, i: (0, i, h))
    stat = pl.BlockSpec((1, tops, size, 1), lambda h, i: (h, 0, i, 0))
    return keys, own, two, stat

def attend_prompt(q, k, v, tile=256):
    tops, rows, width = q.shape; heads = width // HD
    by_head, two, stat = prompt_specs(tops, rows)
    return pl.pallas_call(functools.partial(prompt_fwd, tile), grid=(heads,), in_specs=[two, by_head, by_head], out_specs=[two, stat],
        out_shape=[jax.ShapeDtypeStruct(q.shape, BF16), jax.ShapeDtypeStruct((heads, tops, rows, 1), F32)],
        compiler_params=kernel_params(1, 48), cost_estimate=cost(tops, rows, rows//2, width, 1), name="attend_prompt")(q, k, v)

def attend_cont(q, kp, vp, k, v, length, earlier):
    tops, rows, width = q.shape; heads = width // HD; size = 2*length
    keys, own, two, stat = cont_specs(tops, kp.shape[0], size)
    return pl.pallas_call(functools.partial(cont_fwd, length), grid=(heads, rows//size), in_specs=[two, keys, keys, own, own, anywhere()], out_specs=[two, stat],
        out_shape=[jax.ShapeDtypeStruct(q.shape, BF16), jax.ShapeDtypeStruct((heads, tops, rows, 1), F32)],
        compiler_params=kernel_params(2, 48), cost_estimate=cost(tops, rows, kp.shape[0], width, 1), name="attend_cont")(q, kp, vp, k, v, earlier)

def attend_prompt_back(q, k, v, do, lse, tile=256):
    tops, rows, width = q.shape; heads = width // HD
    by_head, two, stat = prompt_specs(tops, rows)
    return pl.pallas_call(functools.partial(prompt_bwd, tile), grid=(heads,), in_specs=[two, by_head, by_head, two, stat], out_specs=[two, by_head, by_head],
        out_shape=[jax.ShapeDtypeStruct(q.shape, BF16)] + [jax.ShapeDtypeStruct(k.shape, F32)]*2,
        compiler_params=kernel_params(1, 48), cost_estimate=cost(tops, rows, rows//2, width, 3), name="attend_prompt_back")(q, k, v, do, lse)

def attend_cont_back(q, kp, vp, k, v, do, lse, dkp, dvp, length):
    tops, rows, width = q.shape; heads = width // HD; size = 2*length
    keys, own, two, stat = cont_specs(tops, kp.shape[0], size)
    return pl.pallas_call(functools.partial(cont_bwd, length), grid=(heads, rows//size), in_specs=[two, keys, keys, own, own, two, stat, keys, keys], out_specs=[two, keys, keys, own, own],
        out_shape=[jax.ShapeDtypeStruct(m.shape, BF16) for m in (q, kp, kp, k, k)], scratch_shapes=[pltpu.VMEM((kp.shape[0], HD), F32)]*2,
        compiler_params=kernel_params(2, 48), cost_estimate=cost(tops, rows, kp.shape[0], width, 3), name="attend_cont_back")(q, kp, vp, k, v, do, lse, dkp, dvp)


def on_device(
    prompt_in,
    cont_in,
    cotan_prompt,
    cotan_cont,
    routes_attn_p,
    routes_attn_c,
    routes_ffn_p,
    routes_ffn_c,
    adapter_pick,
    norm_gains,
    router_attn,
    router_ffn,
    w_kv,
    w_query,
    w_out,
    w_gate_up,
    w_down,
    ada_in,
    ada_out,
    ada_down,
    ada_ffn,
):
    features = prompt_in.shape[2]
    n_attn = w_query.shape[0]
    n_ffn = w_down.shape[0]
    shards = lax.axis_size("shard")
    reps = lax.axis_size("rep")
    rep_id = lax.axis_index("rep")
    shard_id = lax.axis_index("shard")
    hops = range(1, shards)
    cont_len = cont_in.shape[2]
    sizes = (prompt_in.shape[1], cont_in.shape[1] * cont_len)
    width = w_kv.shape[2]
    both = range(2)
    rank = ada_in.shape[2]
    tops = routes_attn_p.shape[2]

    def tie(values, earlier):
        return values + (earlier[(0,) * earlier.ndim] * 0).astype(values.dtype)

    def gather(values):
        return lax.all_gather(values, "shard", axis=0)

    def scatter(values):
        return lax.psum_scatter(values, "shard", scatter_dimension=0, tiled=True)

    def spread_blocks(values):
        block = lambda t: lax.dynamic_index_in_dim(values, t % shards, 0, keepdims=False)
        out = [block(shard_id)]
        for hop in hops:
            pairs = [(k, (k + hop) % shards) for k in range(shards)]
            out.append(lax.ppermute(block(shard_id + hop), "shard", pairs))
        return out

    def in_order(by_distance):
        out = []
        for t in range(shards):
            value = by_distance[0]
            for hop in hops:
                value = jnp.where((shard_id - hop) % shards == t, by_distance[hop], value)
            out.append(value)
        return out

    def cube_gather(values, axis):
        shape, bit, place = values.shape, reps // 2, axis
        while bit:
            other = lax.ppermute(values, "rep", [(k, k ^ bit) for k in range(reps)])
            high = (rep_id // bit) % 2 == 1
            values = jnp.stack(
                [jnp.where(high, other, values), jnp.where(high, values, other)], axis=place
            )
            bit, place = bit // 2, place + 1
        return values.reshape(shape[:axis] + (reps,) + shape[axis:])

    flat = lambda m: m[0].reshape(-1, m.shape[-1])
    x_own = [flat(prompt_in), flat(cont_in)]
    c_own = [flat(cotan_prompt), flat(cotan_cont)]
    ra_own = [flat(routes_attn_p), flat(routes_attn_c)]
    rf_own = [flat(routes_ffn_p), flat(routes_ffn_c)]
    chosen = adapter_pick[0]
    own_in = lax.dynamic_index_in_dim(ada_in, chosen, 0, keepdims=False)
    own_out = lax.dynamic_index_in_dim(ada_out, chosen, 0, keepdims=False)
    own_down = lax.dynamic_index_in_dim(ada_down, chosen, 0, keepdims=False)
    own_ffn = lax.dynamic_index_in_dim(ada_ffn, chosen, 0, keepdims=False)
    gain_one = norm_gains[0].astype(F32)
    gain_two = norm_gains[1].astype(F32)

    factors = jnp.concatenate([own_in[:3], own_in[4:6], own_out[3:5]], axis=0)
    routes = jnp.concatenate([jnp.concatenate(m, axis=0) for m in (ra_own, rf_own)], axis=1)
    extra = jnp.concatenate([factors.reshape(-1), routes.astype(BF16).reshape(-1)])
    extra_rows = -(-extra.size // (16 * features)) * 16
    extra = jnp.pad(extra, (0, extra_rows * features - extra.size)).reshape(extra_rows, features)
    n1_own, r1, wa_own = [], [], []
    for i in both:
        normed, inverse = norm_rows(x_own[i].astype(F32), gain_one)
        normed = normed.astype(BF16)
        n1_own.append(normed)
        r1.append(inverse)
        wa_own.append(route_shares(dot32(normed, router_attn), ra_own[i]))
    sent = jnp.concatenate(n1_own + [extra], axis=0)
    load = gather(sent)
    spans = [(0, sizes[0]), sizes]
    extra = load[:, sum(sizes) :].reshape(shards, -1)
    full = extra[:, : factors.size].reshape((shards,) + factors.shape)
    full = full.transpose(1, 2, 0, 3).reshape(factors.shape[:2] + (-1,))
    a_qkv = jnp.concatenate([full[:3].reshape(3 * rank, features), router_attn.T], axis=0)
    a_ff = full[3:5].reshape(2 * rank, features)
    b_o, b_down = full[5], full[6]
    b_qkv, a_o = own_out[:3], own_in[3]
    routes = extra[:, factors.size : factors.size + routes.size].reshape((shards,) + routes.shape)
    rf = [routes[:, spans[i][0] : sum(spans[i]), tops:].astype(jnp.int32) for i in both]
    rf = [m.reshape(-1, tops) for m in rf]
    hot = [slot_onehots(rf[i], n_ffn, sizes[i]) for i in both]
    routes = jnp.pad(routes, ((0, 0), (0, 0), (0, EXT - 2 * tops)))
    piece = width // reps
    mine = lax.dynamic_index_in_dim(
        w_out.reshape(n_attn, shards, reps, piece, w_out.shape[2]), rep_id, 2, keepdims=False
    )
    turned = spread_blocks(tie(mine.transpose(1, 0, 2, 3), sent))
    turned = jnp.concatenate(in_order(turned), axis=2)
    w_o = cube_gather(turned, 1).reshape(n_attn, width, features)

    q, k, v, low1 = [None, None], [None, None], [None, None], [None, None]
    for i in both:
        q[i], k[i], v[i], low1[i] = qkv_call(load, routes, spans[i], tops, w_query, w_kv, a_qkv, b_qkv)
    o, lse = [None, None], [None, None]
    o[0], lse[0] = attend_prompt(q[0], k[0], v[0])
    o[1], lse[1] = attend_cont(q[1], k[0], v[0], k[1], v[1], cont_len, o[0])
    partial = []
    for i in both:
        partial.append(out_call(low1[i], sizes[i], o[i], w_o, a_o, b_o))
    c_load = [gather(tie(c_own[0], load))]
    partial[0] = tie(partial[0], c_load[0])
    h1, n2_own, r2, wf_own, n2 = [], [], [], [], []
    for i in both:
        hidden = x_own[i].astype(F32) + scatter(partial[i]).astype(F32)
        normed, inverse = norm_rows(hidden, gain_two)
        normed = normed.astype(BF16)
        h1.append(hidden)
        r2.append(inverse)
        n2_own.append(normed)
        wf_own.append(route_shares(dot32(normed, router_ffn), rf_own[i]))
        by_expert = jnp.sum(wf_own[i][:, :, None] * hits(rf_own[i], n_ffn), axis=1)
        low = dot_nt(normed, a_ff)
        columns = split_low(low[:, :rank]) + split_low(low[:, rank:]) + split_low(by_expert)
        n2_sent = with_ext(normed, columns)
        n2.append(gather(n2_sent if i else tie(n2_sent, partial[1])))
    c_last = tie(c_own[1], n2_own[1])
    c_load.append(gather(c_last))
    c_raw = c_load[1]
    for i in both:
        low = split_low(dot_nt(c_load[i].reshape(-1, features), b_down))
        c_load[i] = with_ext(c_load[i].reshape(-1, features), low).reshape(shards, -1, features + EXT)

    blank = jnp.zeros((2 * rank, own_down.shape[1]), BF16)
    fac_gu = [twice(own_ffn[0]), blank], [blank, twice(own_ffn[1])]
    fac_gu = jnp.stack([jnp.concatenate(m + [blank] * (EXT // (2 * rank) - 2), axis=0) for m in fac_gu])
    fac_d = jnp.concatenate([twice(own_down)] + [blank] * (EXT // (2 * rank) - 1), axis=0).T
    half = n_ffn // 2
    y_slots, dx, sums = [[], []], [[], []], []

    def run_experts(i, part, earlier):
        one, two, three = ffn_call(
            hot[i],
            n2[i],
            c_load[i],
            w_gate_up,
            w_down,
            fac_gu,
            fac_d,
            rank,
            earlier,
            part * half,
            half,
        )
        y_slots[i].append(one)
        dx[i].append(two)
        sums.append(three)

    dh1, dh_sent, dh_load, d_partial, y_partial, y_own = [], [], [], [], [], []
    g_a_ff, g_b_down = [], []

    def sum_rows(i):
        lows = (0, 2 * rank)
        out, part = rows_call(hot[i], dx[i], n2[i], a_ff, lows, True, c_raw)
        g_a_ff.append(part)
        d_partial.append(tie(out, dh_load[0]) if i else out)
        out, part = rows_call(hot[i], y_slots[i], c_load[i], b_down, (0,), False, out)
        g_b_down.append(part)
        y_partial.append(out)

    def send_back(i, earlier):
        rows = scatter(d_partial[i])
        d_rows, ext = rows[:, :features].astype(F32), rows[:, features:]
        dw_own = ext[:, None, 4 * rank : 4 * rank + n_ffn].astype(F32)
        dw_top = jnp.sum(hits(rf_own[i], n_ffn) * dw_own, axis=2)
        d_logits = shares_back(wf_own[i], rf_own[i], n_ffn, dw_top)
        d_rows = d_rows + exact_mm(d_logits, router_ffn.astype(F32).T)
        dh1.append(c_own[i].astype(F32) + norm_back(h1[i], r2[i], gain_two, d_rows))
        dh_sent.append(tie(dh1[i], earlier).astype(BF16))
        dh_load.append(gather(dh_sent[i]))

    run_experts(0, 0, c_last)
    run_experts(0, 1, n2[1])
    sum_rows(0)
    run_experts(1, 0, y_partial[0])
    send_back(0, dx[1][0])
    run_experts(1, 1, dh_sent[0])
    sum_rows(1)

    do, dwa, dq, dk, dv = ([None, None] for _ in range(5))
    g_a_o = jnp.zeros(a_o.shape, F32)
    g_b_o = jnp.zeros(b_o.shape, F32)
    for i in both:
        if i:
            send_back(1, dq[0])
        do[i], dwa[i], part_a, part_b = out_back_call(
            low1[i], sizes[i], dh_load[i], o[i], w_o, a_o, b_o
        )
        g_a_o, g_b_o = g_a_o + part_a, g_b_o + part_b
        if i:
            dq[1], dk[0], dv[0], dk[1], dv[1] = attend_cont_back(
                q[1], k[0], v[0], k[1], v[1], do[1], lse[1], dkp, dvp, cont_len
            )
        else:
            dq[0], dkp, dvp = attend_prompt_back(q[0], k[0], v[0], do[0], lse[0])
    y_sent = tie(y_partial[0], dh_load[1])
    y_own.append(scatter(y_sent))
    y_own.append(scatter(tie(y_partial[1], y_own[0])))
    outs = [(h1[i] + y_own[i].astype(F32)).astype(BF16) for i in both]
    g_units, g_a_ff, g_b_down = sum(sums), sum(g_a_ff), sum(g_b_down)

    g_a_qkv = jnp.zeros((3 * rank, features), F32)
    g_b_qkv = jnp.zeros(b_qkv.shape, F32)
    grads = []
    earlier = (y_sent,)
    for i in both:
        rows, part_a, part_b = qkv_back_call(
            load,
            spans[i],
            dq[i],
            dk[i],
            dv[i],
            dwa[i],
            low1[i],
            w_query,
            w_kv,
            b_qkv,
            earlier,
        )
        earlier = (rows, y_own[0])
        g_a_qkv, g_b_qkv = g_a_qkv + part_a, g_b_qkv + part_b
        rows = scatter(rows)
        d_rows, ext = rows[:, :features].astype(F32), rows[:, features:]
        d_logits = shares_back(wa_own[i], ra_own[i], n_attn, ext[:, :tops].astype(F32))
        d_rows = d_rows + dot32(ext[:, rank : 4 * rank], a_qkv[: 3 * rank])
        d_rows = d_rows + exact_mm(d_logits, router_attn.astype(F32).T)
        grads.append(dh1[i] + norm_back(x_own[i].astype(F32), r1[i], gain_one, d_rows))
    adapters = ada_in.shape[0]
    pick_lines = jnp.broadcast_to(adapter_pick.astype(BF16)[:, None], (16, 128))

    partial = jnp.concatenate([g_a_qkv, g_a_ff, g_b_o, g_b_down], axis=0).astype(BF16)
    partial = partial.reshape(-1, shards, width).transpose(1, 0, 2)
    summed = sum(m.astype(F32) for m in spread_blocks(partial)).reshape(-1, rank, width)
    grads_own = [summed[:3], g_a_o[None], summed[3:5], g_b_qkv, summed[5:], g_units]
    lines = [g.astype(BF16).reshape(-1, 128) for g in grads_own]
    every = cube_gather(jnp.concatenate([pick_lines] + lines, axis=0), 0)
    picks = every[:, 0, 0].astype(F32)
    by_adapter = (picks[None, :] == jnp.arange(adapters, dtype=F32)[:, None]).astype(F32)
    total = jnp.sum(by_adapter[:, :, None, None] * every.astype(F32)[None], axis=1)
    out, start = [], pick_lines.shape[0]
    for line, grad in zip(lines, grads_own):
        out.append(total[:, start : start + line.shape[0]].reshape((adapters,) + grad.shape))
        start += line.shape[0]
    g_in = jnp.concatenate(out[:3], axis=1)
    g_out = jnp.concatenate(out[3:5], axis=1)

    shape_c = (1,) + cont_in.shape[1:]
    return (
        outs[0][None],
        outs[1].reshape(shape_c),
        grads[0][None],
        grads[1].reshape(shape_c),
        g_in,
        g_out,
        out[5][:, 2],
        out[5][:, :2],
    )


def solution(mesh):
    rows = (P("rep", "shard", None), P("rep", "shard", None, None))
    last = (
        P(None, None, None, "shard"),
        P(None, None, None, "shard"),
        P(None, None, "shard"),
        P(None, None, None, "shard"),
    )
    in_specs = (
        rows * 4
        + (P("rep"), P(), P(), P())
        + (P(None, None, "shard"),) * 3
        + (P(None, None, None, "shard"), P(None, "shard", None))
        + last
    )
    return jax.shard_map(
        on_device, mesh=mesh, in_specs=in_specs, out_specs=rows * 2 + last, check_vma=False
    )
```

```python
import functools

import jax
import jax.numpy as jnp
from jax import lax
from jax.experimental import pallas as pl
from jax.experimental.pallas import tpu as pltpu
from jax.sharding import PartitionSpec as P

HD = 128
SCALE = HD**-0.5
EPSILON = 1e-05
HIGHEST = lax.Precision.HIGHEST
F32 = jnp.float32
BF16 = jnp.bfloat16
EXT = 128


def dot32(former, latter):
    return jnp.dot(former, latter, preferred_element_type=F32)


def dot_nt(former, latter):
    return lax.dot_general(former, latter, (((1,), (1,)), ((), ())), preferred_element_type=F32)


def dot_tn(former, latter):
    return lax.dot_general(former, latter, (((0,), (0,)), ((), ())), preferred_element_type=F32)


def exact_mm(former, latter):
    return jnp.dot(former, latter, precision=HIGHEST)


def split_low(values):
    high = values.astype(BF16)
    return [high, (values - high.astype(F32)).astype(BF16)]


def twice(values):
    return jnp.concatenate([values, values], axis=0)


def norm_rows(values, scaling):
    inverse = lax.rsqrt(jnp.mean(values * values, axis=-1, keepdims=True) + EPSILON)
    return (values * inverse * scaling, inverse)


def norm_back(values, inverse, scaling, upstream):
    weighted = upstream * scaling
    inner_mean = jnp.mean(weighted * values, axis=-1, keepdims=True)
    return inverse * weighted - values * (inverse * inverse * inverse) * inner_mean


def capacity(block_rows, experts, top_count):
    return min(block_rows, ((block_rows * top_count + experts - 1) // experts + 7) // 8 * 8 + 8)


def hits(routes, experts):
    labels = jnp.arange(experts, dtype=jnp.int32)
    return (routes[:, :, None] == labels[None, None, :]).astype(F32)


def slot_onehots(routes, experts, block):
    rows, top_count = routes.shape
    slot_cap = capacity(block, experts, top_count)
    member = jnp.sum(hits(routes, experts), axis=1).reshape(-1, 2, block, experts)
    place = jnp.arange(block, dtype=jnp.int32)
    before = (place[None, :] < place[:, None]).astype(BF16)
    ranked = jnp.einsum("rq,phqe->phre", before, member.astype(BF16), preferred_element_type=F32)
    ranked = ranked + jnp.arange(2, dtype=F32)[None, :, None, None] * slot_cap
    slot_of = jnp.where(member > 0, ranked, -1.0).reshape(-1, 2 * block, experts)
    slots = jnp.arange(2 * slot_cap, dtype=F32)
    return (slot_of.transpose(2, 0, 1)[:, :, None, :] == slots[None, None, :, None]).astype(BF16)


def route_shares(logits, routes):
    chosen = jnp.einsum("rte,re->rt", hits(routes, logits.shape[1]), logits, precision=HIGHEST)
    return jax.nn.softmax(chosen, axis=-1)


def shares_back(shares, routes, experts, d_shares):
    d_chosen = shares * (d_shares - jnp.sum(shares * d_shares, axis=-1, keepdims=True))
    return jnp.sum(d_chosen[:, :, None] * hits(routes, experts), axis=1)


def with_ext(rows, columns):
    used = sum(c.shape[1] for c in columns)
    columns = [c.astype(BF16) for c in columns]
    blank = jnp.zeros((rows.shape[0], EXT - used), BF16)
    return jnp.concatenate([rows.astype(BF16)] + columns + [blank], axis=1)


def whole(*shape):
    return pl.BlockSpec(
        shape, lambda *ids: (0,) * len(shape), pipeline_mode=pl.Buffered(buffer_count=1)
    )


def anywhere():
    return pl.BlockSpec(memory_space=pl.ANY)


def kernel_params(dims, mib):
    return pltpu.CompilerParams(
        dimension_semantics=("arbitrary",) * dims, vmem_limit_bytes=mib * 2**20
    )


def pair_rows(ref, span):
    start, rows = span
    return ref[:, start : start + rows, :].reshape(2 * rows, ref.shape[2])


def ext_choice(ext, tops, experts, rank):
    ext = ext[...].astype(F32)
    at = 3 * rank
    shares = [ext[:, at + t : at + t + 1] + ext[:, at + tops + t : at + tops + t + 1] for t in range(tops)]
    at = at + 2 * tops
    chosen = [[ext[:, at + t : at + t + 1] == e for e in range(experts)] for t in range(tops)]
    return shares, chosen


def qkv_kernel(span, tops, rank, load, routes, w_q, w_kv, fac_a, fac_b, q, k, v, low_out):
    features = w_q.shape[1]
    experts = w_q.shape[0]
    rows = span[1]
    block = pair_rows(load, span)
    n1 = block
    route = pair_rows(routes, span)[:, :tops].astype(F32)
    chosen = [[route[:, t : t + 1] == e for e in range(experts)] for t in range(tops)]
    low = dot_nt(n1, fac_a[...])
    logits = [
        sum(jnp.where(chosen[t][e], low[:, 3 * rank + e : 3 * rank + e + 1], 0.0) for e in range(experts))
        for t in range(tops)
    ]
    peak = functools.reduce(jnp.maximum, logits)
    shares = [jnp.exp(m - peak) for m in logits]
    total = sum(shares)
    shares = split_low(jnp.concatenate([m / total for m in shares], axis=1))
    low_out[...] = jnp.concatenate(
        [low[:, : 3 * rank].astype(BF16)]
        + shares
        + [route.astype(BF16), jnp.zeros((2 * rows, EXT - 3 * rank - 3 * tops), BF16)],
        axis=1,
    )
    shift = []
    for j in range(3):
        wide = jnp.concatenate(split_low(low[:, rank * j : rank * (j + 1)]), axis=1)
        shift.append(dot32(wide, twice(fac_b[j])))
    k[...] = (dot32(n1, w_kv[0]) + shift[1]).astype(BF16)
    v[...] = (dot32(n1, w_kv[1]) + shift[2]).astype(BF16)
    picked = [shift[0]] * tops
    for e in range(experts):
        here = dot32(n1, w_q[e])
        for t in range(tops):
            picked[t] = picked[t] + jnp.where(chosen[t][e], here, 0.0)
    for t in range(tops):
        q[t] = picked[t].astype(BF16)


def qkv_call(load, routes, span, tops, w_q, w_kv, fac_a, fac_b):
    shards, held, wide = load.shape
    rows = span[1]
    width = w_q.shape[2]
    total = shards * rows
    rank = fac_b.shape[1]
    out = lambda n: pl.BlockSpec((2 * rows, n), lambda p: (p, 0))
    return pl.pallas_call(
        functools.partial(qkv_kernel, span, tops, rank),
        grid=(shards // 2,),
        in_specs=[
            pl.BlockSpec((2, held, wide), lambda p: (p, 0, 0)),
            pl.BlockSpec((2,) + routes.shape[1:], lambda p: (p, 0, 0)),
            whole(*w_q.shape),
            whole(*w_kv.shape),
            whole(*fac_a.shape),
            whole(*fac_b.shape),
        ],
        out_specs=[
            pl.BlockSpec((tops, 2 * rows, width), lambda p: (0, p, 0)),
            out(width),
            out(width),
            out(EXT),
        ],
        out_shape=[
            jax.ShapeDtypeStruct((tops, total, width), BF16),
            jax.ShapeDtypeStruct((total, width), BF16),
            jax.ShapeDtypeStruct((total, width), BF16),
            jax.ShapeDtypeStruct((total, EXT), BF16),
        ],
        compiler_params=kernel_params(1, 56),
        cost_estimate=pl.CostEstimate(
            flops=2 * total * w_q.shape[1] * width * (w_q.shape[0] + 2),
            bytes_accessed=2 * (w_q.size + w_kv.size + load.size),
            transcendentals=0,
        ),
        name="qkv",
    )(load, routes, w_q, w_kv, fac_a, fac_b)


def out_kernel(tops, ext, o, w_o, fac_a, fac_b, out):
    experts = w_o.shape[0]
    shares, chosen = ext_choice(ext, tops, experts, fac_a.shape[0])
    parts = [o[t].astype(F32) * shares[t] for t in range(tops)]
    low = dot_nt(sum(parts).astype(BF16), fac_a[...])
    total = dot32(jnp.concatenate(split_low(low), axis=1), twice(fac_b[...]))
    for e in range(experts):
        here = sum(jnp.where(chosen[t][e], parts[t], 0.0) for t in range(tops)).astype(BF16)
        total = total + dot32(here, w_o[e])
    out[...] = total.astype(BF16)


def out_call(ext, rows, o, w_o, fac_a, fac_b):
    tops, total, width = o.shape
    features = w_o.shape[2]
    return pl.pallas_call(
        functools.partial(out_kernel, tops),
        grid=(total // (2 * rows),),
        in_specs=[
            pl.BlockSpec((2 * rows, EXT), lambda p: (p, 0)),
            pl.BlockSpec((tops, 2 * rows, width), lambda p: (0, p, 0)),
            whole(*w_o.shape),
            whole(*fac_a.shape),
            whole(*fac_b.shape),
        ],
        out_specs=pl.BlockSpec((2 * rows, features), lambda p: (p, 0)),
        out_shape=jax.ShapeDtypeStruct((total, features), BF16),
        compiler_params=kernel_params(1, 56),
        cost_estimate=pl.CostEstimate(
            flops=2 * total * w_o.size,
            bytes_accessed=2 * (w_o.size + o.size + total * features),
            transcendentals=0,
        ),
        name="project_out",
    )(ext, o, w_o, fac_a, fac_b)


def out_back_kernel(tops, ext, dh, o, w_o, fac_a, fac_b, do, dw, grad_a, grad_b):
    experts = w_o.shape[0]
    shares, chosen = ext_choice(ext, tops, experts, fac_a.shape[0])
    block = dh[...].reshape(-1, dh.shape[2])
    rows = block.shape[0]
    low = split_low(dot_nt(block, fac_b[...]))
    shift = dot32(jnp.concatenate(low, axis=1), twice(fac_a[...]))
    picked = [shift] * tops
    for e in range(experts):
        here = dot_nt(block, w_o[e])
        for t in range(tops):
            picked[t] = picked[t] + jnp.where(chosen[t][e], here, 0.0)
    lane = lax.broadcasted_iota(jnp.int32, (rows, EXT), 1)
    back = jnp.zeros((rows, EXT), F32)
    total = None
    for t in range(tops):
        value = o[t].astype(F32)
        back = back + jnp.where(lane == t, jnp.sum(picked[t] * value, axis=1, keepdims=True), 0.0)
        do[t] = (picked[t] * shares[t]).astype(BF16)
        value = value * shares[t]
        total = value if total is None else total + value
    dw[...] = back.astype(BF16)
    total = total.astype(BF16)

    @pl.when(pl.program_id(0) == 0)
    def _():
        grad_a[...] = jnp.zeros_like(grad_a)
        grad_b[...] = jnp.zeros_like(grad_b)

    grad_a[...] += dot_tn(low[0], total)
    grad_b[...] += dot_tn(dot_nt(total, fac_a[...]).astype(BF16), block)


def out_back_call(ext, rows, dh, o, w_o, fac_a, fac_b):
    tops, total, width = o.shape
    rank, features = fac_b.shape
    two = pl.BlockSpec((tops, 2 * rows, width), lambda p: (0, p, 0))
    row = pl.BlockSpec((2 * rows, EXT), lambda p: (p, 0))
    return pl.pallas_call(
        functools.partial(out_back_kernel, tops),
        grid=(total // (2 * rows),),
        in_specs=[
            row,
            pl.BlockSpec((2,) + dh.shape[1:], lambda p: (p, 0, 0)),
            two,
            whole(*w_o.shape),
            whole(*fac_a.shape),
            whole(*fac_b.shape),
        ],
        out_specs=[
            two,
            row,
            pl.BlockSpec((rank, width), lambda p: (0, 0)),
            pl.BlockSpec((rank, features), lambda p: (0, 0)),
        ],
        out_shape=[
            jax.ShapeDtypeStruct(o.shape, BF16),
            jax.ShapeDtypeStruct((total, EXT), BF16),
            jax.ShapeDtypeStruct((rank, width), F32),
            jax.ShapeDtypeStruct((rank, features), F32),
        ],
        compiler_params=kernel_params(1, 56),
        cost_estimate=pl.CostEstimate(
            flops=2 * total * w_o.size,
            bytes_accessed=2 * (w_o.size + 2 * o.size + total * features),
            transcendentals=0,
        ),
        name="project_out_back",
    )(ext, dh, o, w_o, fac_a, fac_b)


def qkv_back_kernel(span, tops, rank, load, dq, dk, dv, low_in, w_q, w_kv, fac_b, fac_a, out, grad_a, grad_b):
    experts, features, _ = w_q.shape
    rows = span[1]
    block = pair_rows(load, span)
    _, chosen = ext_choice(low_in, tops, experts, rank)
    total = dot_nt(dk[...], w_kv[0]) + dot_nt(dv[...], w_kv[1])
    blank = jnp.zeros(dk.shape, BF16)
    for e in range(experts):
        here = blank
        for t in range(tops):
            here = jnp.where(chosen[t][e], dq[t], here)
        total = total + dot_nt(here, w_q[e])
    dq_sum = sum(dq[t].astype(F32) for t in range(tops)).astype(BF16)
    sides = [dq_sum, dk[...], dv[...]]
    low = jnp.concatenate([dot_nt(sides[j], fac_b[j]) for j in range(3)], axis=1)
    total = total + dot32(jnp.concatenate(split_low(low), axis=1), twice(fac_a[...]))
    out[...] = total.astype(BF16)

    @pl.when(pl.program_id(0) == 0)
    def _():
        grad_a[...] = jnp.zeros_like(grad_a)
        grad_b[...] = jnp.zeros_like(grad_b)

    grad_a[...] += dot_tn(low.astype(BF16), block)
    for j in range(3):
        grad_b[j] += dot_tn(low_in[:, rank * j : rank * (j + 1)], sides[j])


def qkv_back_call(load, span, dq, dk, dv, low_in, w_q, w_kv, fac_b, fac_a, earlier):
    tops, total, width = dq.shape
    rows = span[1]
    features = w_q.shape[1]
    rank = fac_b.shape[1]
    row = lambda n: pl.BlockSpec((2 * rows, n), lambda p: (p, 0))

    def kernel(*refs):
        qkv_back_kernel(span, tops, rank, *refs[:9], *refs[9 + len(earlier) :])

    return pl.pallas_call(
        kernel,
        grid=(total // (2 * rows),),
        in_specs=[
            pl.BlockSpec((2,) + load.shape[1:], lambda p: (p, 0, 0)),
            pl.BlockSpec((tops, 2 * rows, width), lambda p: (0, p, 0)),
            row(width),
            row(width),
            row(EXT),
            whole(*w_q.shape),
            whole(*w_kv.shape),
            whole(*fac_b.shape),
            whole(*fac_a.shape),
        ]
        + [anywhere() for _ in earlier],
        out_specs=[
            row(features),
            pl.BlockSpec((3 * rank, features), lambda p: (0, 0)),
            pl.BlockSpec((3, rank, width), lambda p: (0, 0, 0)),
        ],
        out_shape=[
            jax.ShapeDtypeStruct((total, features), BF16),
            jax.ShapeDtypeStruct((3 * rank, features), F32),
            jax.ShapeDtypeStruct((3, rank, width), F32),
        ],
        compiler_params=kernel_params(1, 56),
        cost_estimate=pl.CostEstimate(
            flops=2 * total * (w_q.size + w_kv.size),
            bytes_accessed=2 * (w_q.size + w_kv.size + 2 * load.size),
            transcendentals=0,
        ),
        name="qkv_back",
    )(load, dq, dk, dv, low_in, w_q, w_kv, fac_b, fac_a, *earlier)


def ffn_tiles(units):
    if units % 128:
        return [(0, units)]
    return [(start, min(512, units - start)) for start in range(0, units, 512)]


def ffn_kernel(tiles, rank, begin, hot, n2, c, w_gu, w_d, fac_gu, fac_d, y_out, dx_out, g_out, xs, cs, acc_y, acc_d, buf_gu, buf_d, sems):
    e = pl.program_id(0)
    here = pl.num_programs(0)
    experts, _, features = w_d.shape
    count = len(tiles)
    pairs, slots, _ = hot.shape[1:]
    rows = n2.shape[1]
    total = pairs * slots
    side = pl.ds(features, EXT)

    def copies(expert, t, slot):
        start, size = tiles[t]
        cols = pl.ds(start, size)
        got = pl.ds(0, size)
        pairs_of = [
            (w_gu.at[begin + expert, 0, :, cols], buf_gu.at[slot, 0, pl.ds(0, features), got]),
            (w_gu.at[begin + expert, 1, :, cols], buf_gu.at[slot, 1, pl.ds(0, features), got]),
            (w_d.at[begin + expert, cols, :], buf_d.at[slot, got, pl.ds(0, features)]),
            (fac_gu.at[:, :, cols], buf_gu.at[slot, :, side, got]),
            (fac_d.at[cols, :], buf_d.at[slot, got, side]),
        ]
        return [pltpu.make_async_copy(*m, sems.at[slot, n]) for n, m in enumerate(pairs_of)]

    @pl.when(e == 0)
    def _():
        for m in copies(0, 0, 0):
            m.start()
        g_out[...] = jnp.zeros_like(g_out)

    for p in range(pairs):
        spot = pl.ds(p * slots, slots)
        xs[spot, :] = dot32(hot[0, p], n2[2 * p : 2 * p + 2].reshape(2 * rows, -1)).astype(BF16)
        cs[spot, :] = dot32(hot[0, p], c[2 * p : 2 * p + 2].reshape(2 * rows, -1)).astype(BF16)
    lane = lax.broadcasted_iota(jnp.int32, (total, EXT), 1)
    ext = xs[:, features:]
    mine = (lane == 4 * rank + begin + e) | (lane == 4 * rank + experts + begin + e)
    share = jnp.sum(jnp.where(mine, ext.astype(F32), 0.0), axis=1, keepdims=True)
    low = [ext[:, :rank], ext[:, 2 * rank : 3 * rank], cs[:, features : features + rank]]
    low[2] = (low[2].astype(F32) * share).astype(BF16)
    dw = None
    for t, (start, size) in enumerate(tiles):
        slot = lax.rem(e * count + t, 2)
        for m in copies(e, t, slot):
            m.wait()
        if t + 1 < count:
            for m in copies(e, t + 1, 1 - slot):
                m.start()
        else:

            @pl.when(e + 1 < here)
            def _():
                for m in copies(e + 1, 0, 1 - slot):
                    m.start()

        spot = pl.ds(0, size)
        cols = pl.ds(start, size)
        wg, wu, wd = buf_gu.at[slot, 0, :, spot], buf_gu.at[slot, 1, :, spot], buf_d.at[slot, spot, :]
        g0 = dot32(xs[...], wg[...])
        g1 = dot32(xs[...], wu[...])
        da = dot_nt(cs[...], wd[...])
        sig = 1.0 / (1.0 + jnp.exp(-g0))
        silu = g0 * sig
        act = (silu * g1).astype(BF16)
        now = jnp.sum(da * act.astype(F32), axis=1, keepdims=True)
        dw = now if dw is None else dw + now
        da = da * share
        dg0 = (da * g1 * (sig + silu * (1.0 - sig))).astype(BF16)
        dg1 = (da * silu).astype(BF16)
        g_out[0, :, cols] += dot_tn(low[0], dg0)
        g_out[1, :, cols] += dot_tn(low[1], dg1)
        g_out[2, :, cols] += dot_tn(low[2], act)
        if t == 0 and count > 1:
            acc_y[...] = dot32(act, wd[...])
            acc_d[...] = dot_nt(dg0, wg[...]) + dot_nt(dg1, wu[...])
        elif t + 1 < count:
            acc_y[...] += dot32(act, wd[...])
            acc_d[...] += dot_nt(dg0, wg[...]) + dot_nt(dg1, wu[...])
        else:
            y = dot32(act, wd[...])
            d = dot_nt(dg0, wg[...]) + dot_nt(dg1, wu[...])
            if count > 1:
                y, d = y + acc_y[...], d + acc_d[...]
            y_out[0] = (y * share).astype(BF16)
            dx_out[0] = d.astype(BF16)
            d = jnp.where(lane == 4 * rank + begin + e, dw, d[:, features:])
            dx_out[0, :, features:] = d.astype(BF16)


def ffn_call(hot, n2, c, w_gu, w_d, fac_gu, fac_d, rank, earlier, begin, experts):
    _, pairs, slots, _ = hot.shape
    total = pairs * slots
    units, features = w_d.shape[1:]
    wide = features + EXT
    tiles = ffn_tiles(units)
    widest = max(size for _, size in tiles)
    one = lambda *s: pl.BlockSpec((1,) + s, lambda e: (e,) + (0,) * len(s))

    def kernel(*refs):
        ffn_kernel(tiles, rank, begin, *refs[:7], *refs[8:])

    return pl.pallas_call(
        kernel,
        grid=(experts,),
        in_specs=[
            pl.BlockSpec((1,) + hot.shape[1:], lambda e: (begin + e, 0, 0, 0)),
            whole(*n2.shape),
            whole(*c.shape),
        ]
        + [anywhere() for _ in range(5)],
        out_specs=[
            one(total, wide),
            one(total, wide),
            pl.BlockSpec((3, rank, units), lambda e: (0, 0, 0)),
        ],
        out_shape=[
            jax.ShapeDtypeStruct((experts, total, wide), BF16),
            jax.ShapeDtypeStruct((experts, total, wide), BF16),
            jax.ShapeDtypeStruct((3, rank, units), F32),
        ],
        scratch_shapes=[
            pltpu.VMEM((total, wide), BF16),
            pltpu.VMEM((total, wide), BF16),
            pltpu.VMEM((total, wide), F32),
            pltpu.VMEM((total, wide), F32),
            pltpu.VMEM((2, 2, wide, widest), BF16),
            pltpu.VMEM((2, widest, wide), BF16),
            pltpu.SemaphoreType.DMA((2, 5)),
        ],
        compiler_params=kernel_params(1, 62),
        cost_estimate=pl.CostEstimate(
            flops=12 * experts * total * features * units,
            bytes_accessed=6 * experts * features * units + 8 * experts * total * features,
            transcendentals=experts * total * units,
        ),
        name="ffn",
    )(hot, n2, c, w_gu, w_d, fac_gu, fac_d, earlier)


def rows_call(hot, parts, source, fac, lows, keep, earlier):
    experts, pairs, slots, rows = hot.shape
    count, _, wide = parts[0].shape
    rank = fac.shape[0] // len(lows)
    features = wide - EXT
    parts = [m.reshape(count, pairs, slots, wide) for m in parts]
    by_pair = lambda n, *s: pl.BlockSpec((n, 1) + s, lambda p: (0, p, 0, 0))

    def kernel(hot, *refs):
        values, source, fac, _, out, grad = refs[: len(parts)], *refs[len(parts) :]
        total = None
        for e in range(experts):
            here = dot_tn(hot[e, 0], values[e // count][e % count, 0])
            total = here if total is None else total + here
        low = [total[:, features + at : features + at + rank] for at in lows]
        low = split_low(jnp.concatenate(low, axis=1))
        main = total[:, :features] + dot32(jnp.concatenate(low, axis=1), twice(fac[...]))
        out[:, :features] = main.astype(BF16)
        if keep:
            out[:, features:] = total[:, features:].astype(BF16)

        @pl.when(pl.program_id(0) == 0)
        def _():
            grad[...] = jnp.zeros_like(grad)

        grad[...] += dot_tn(low[0], source[:, :, :features].reshape(rows, features))

    out_wide = wide if keep else features
    return pl.pallas_call(
        kernel,
        grid=(pairs,),
        in_specs=[by_pair(experts, slots, rows)]
        + [by_pair(count, slots, wide) for _ in parts]
        + [
            pl.BlockSpec((2,) + source.shape[1:], lambda p: (p, 0, 0)),
            whole(*fac.shape),
            anywhere(),
        ],
        out_specs=[
            pl.BlockSpec((rows, out_wide), lambda p: (p, 0)),
            pl.BlockSpec(fac.shape, lambda p: (0, 0)),
        ],
        out_shape=[
            jax.ShapeDtypeStruct((pairs * rows, out_wide), BF16),
            jax.ShapeDtypeStruct(fac.shape, F32),
        ],
        compiler_params=kernel_params(1, 56),
        cost_estimate=pl.CostEstimate(
            flops=2 * hot.size * wide,
            bytes_accessed=2 * (hot.size + experts * pairs * slots * wide),
            transcendentals=0,
        ),
        name="slots_to_rows",
    )(hot, *parts, source, fac, earlier)


def whole_rows(q):
    return q.reshape(q.shape[0]*q.shape[1], q.shape[2])

def masked_pair(q, keys, diag_keys, seen):
    far = None if keys is None else dot_nt(q, keys)
    near = jnp.where(seen, dot_nt(q, diag_keys), -1e30)
    return far, near

def soft_pair(far, near):
    top = jnp.max(near, axis=1, keepdims=True)
    if far is not None: top = jnp.maximum(top, jnp.max(far, axis=1, keepdims=True))
    p_near = jnp.exp((near - top) * SCALE)
    total = jnp.sum(p_near, axis=1, keepdims=True)
    p_far = None
    if far is not None:
        p_far = jnp.exp((far - top) * SCALE)
        total = total + jnp.sum(p_far, axis=1, keepdims=True)
    return p_far, p_near, top * SCALE + jnp.log(total), 1.0 / total

def prompt_seen(tops, size):
    r = lax.broadcasted_iota(jnp.int32, (tops, size, size), 1).reshape(tops*size, size)
    k = lax.broadcasted_iota(jnp.int32, (tops*size, size), 1)
    return k <= r

def cont_seen(tops, size, length):
    r = lax.broadcasted_iota(jnp.int32, (tops, size, size), 1).reshape(tops*size, size)
    k = lax.broadcasted_iota(jnp.int32, (tops*size, size), 1)
    own = k <= r
    for start in range(length, size, length):
        own = own & ((r < start) | (k >= start))
    return own

def forward_tile(q, far_k, far_v, near_k, near_v, seen):
    far, near = masked_pair(q, far_k, near_k, seen)
    p_far, p_near, lse, inv = soft_pair(far, near)
    o = dot32(p_near.astype(BF16), near_v)
    if far is not None: o = o + dot32(p_far.astype(BF16), far_v)
    return (o * inv).astype(BF16), lse

def prompt_fwd(tile, q, k, v, o, lse):
    tops, rows, _ = q.shape
    for start in range(0, rows, tile):
        here = pl.ds(start, tile)
        out, stat = forward_tile(whole_rows(q[:, here, :]), k[:start, :] if start else None, v[:start, :] if start else None, k[here, :], v[here, :], prompt_seen(tops, tile))
        o[:, here, :] = out.reshape(tops, tile, HD)
        lse[0, :, here, :] = stat.reshape(tops, tile, 1)

def cont_fwd(length, q, kp, vp, k, v, earlier, o, lse):
    tops, size, _ = q.shape
    out, stat = forward_tile(whole_rows(q[...]), kp[...], vp[...], k[...], v[...], cont_seen(tops, size, length))
    o[...] = out.reshape(tops, size, HD)
    lse[0] = stat.reshape(tops, size, 1)

def backward_tile(q, do, lse, far_k, far_v, near_k, near_v, seen):
    far, near = masked_pair(q, far_k, near_k, seen)
    p_near = jnp.exp(near * SCALE - lse)
    dp_near = dot_nt(do, near_v)
    delta = jnp.sum(p_near * dp_near, axis=1, keepdims=True)
    if far is not None:
        p_far = jnp.exp(far * SCALE - lse)
        dp_far = dot_nt(do, far_v)
        delta = delta + jnp.sum(p_far * dp_far, axis=1, keepdims=True)
    ds_near = (p_near * (dp_near - delta)).astype(BF16)
    dq = dot32(ds_near, near_k)
    near_grads = dot_tn(ds_near, q) * SCALE, dot_tn(p_near.astype(BF16), do)
    far_grads = None
    if far is not None:
        ds_far = (p_far * (dp_far - delta)).astype(BF16)
        dq = dq + dot32(ds_far, far_k)
        far_grads = dot_tn(ds_far, q) * SCALE, dot_tn(p_far.astype(BF16), do)
    return (dq * SCALE).astype(BF16), far_grads, near_grads

def prompt_bwd(tile, q, k, v, do, lse, dq, dk, dv):
    tops, rows, _ = q.shape
    for start in range(0, rows, tile):
        here = pl.ds(start, tile)
        out, far, near = backward_tile(whole_rows(q[:, here, :]), whole_rows(do[:, here, :]), lse[0, :, here, :].reshape(tops*tile, 1),
            k[:start, :] if start else None, v[:start, :] if start else None, k[here, :], v[here, :], prompt_seen(tops, tile))
        dq[:, here, :] = out.reshape(tops, tile, HD)
        dk[here, :], dv[here, :] = near
        if start:
            dk[:start, :] += far[0]
            dv[:start, :] += far[1]

def cont_bwd(length, q, kp, vp, k, v, do, lse, dkp_in, dvp_in, dq, dkp, dvp, dk, dv, acc_k, acc_v):
    tops, size, _ = q.shape
    step = pl.program_id(1)
    @pl.when(step == 0)
    def _():
        acc_k[...] = dkp_in[...]
        acc_v[...] = dvp_in[...]
    out, far, near = backward_tile(whole_rows(q[...]), whole_rows(do[...]), lse[0].reshape(tops*size, 1), kp[...], vp[...], k[...], v[...], cont_seen(tops, size, length))
    dq[...] = out.reshape(tops, size, HD)
    dk[...], dv[...] = near[0].astype(BF16), near[1].astype(BF16)
    acc_k[...] += far[0]
    acc_v[...] += far[1]
    @pl.when(step == pl.num_programs(1) - 1)
    def _():
        dkp[...] = acc_k[...].astype(BF16)
        dvp[...] = acc_v[...].astype(BF16)

def cost(tops, rows, keys, width, products):
    return pl.CostEstimate(flops=4*tops*rows*keys*width*products, bytes_accessed=8*rows*width*tops, transcendentals=tops*rows*keys*width//HD)

def prompt_specs(tops, rows):
    by_head = pl.BlockSpec((rows, HD), lambda h: (0, h))
    two = pl.BlockSpec((tops, rows, HD), lambda h: (0, 0, h))
    stat = pl.BlockSpec((1, tops, rows, 1), lambda h: (h, 0, 0, 0))
    return by_head, two, stat

def cont_specs(tops, prompt, size):
    keys = pl.BlockSpec((prompt, HD), lambda h, i: (0, h))
    own = pl.BlockSpec((size, HD), lambda h, i: (i, h))
    two = pl.BlockSpec((tops, size, HD), lambda h, i: (0, i, h))
    stat = pl.BlockSpec((1, tops, size, 1), lambda h, i: (h, 0, i, 0))
    return keys, own, two, stat

def attend_prompt(q, k, v, tile=256):
    tops, rows, width = q.shape; heads = width // HD
    by_head, two, stat = prompt_specs(tops, rows)
    return pl.pallas_call(functools.partial(prompt_fwd, tile), grid=(heads,), in_specs=[two, by_head, by_head], out_specs=[two, stat],
        out_shape=[jax.ShapeDtypeStruct(q.shape, BF16), jax.ShapeDtypeStruct((heads, tops, rows, 1), F32)],
        compiler_params=kernel_params(1, 48), cost_estimate=cost(tops, rows, rows//2, width, 1), name="attend_prompt")(q, k, v)

def attend_cont(q, kp, vp, k, v, length, earlier):
    tops, rows, width = q.shape; heads = width // HD; size = 2*length
    keys, own, two, stat = cont_specs(tops, kp.shape[0], size)
    return pl.pallas_call(functools.partial(cont_fwd, length), grid=(heads, rows//size), in_specs=[two, keys, keys, own, own, anywhere()], out_specs=[two, stat],
        out_shape=[jax.ShapeDtypeStruct(q.shape, BF16), jax.ShapeDtypeStruct((heads, tops, rows, 1), F32)],
        compiler_params=kernel_params(2, 48), cost_estimate=cost(tops, rows, kp.shape[0], width, 1), name="attend_cont")(q, kp, vp, k, v, earlier)

def attend_prompt_back(q, k, v, do, lse, tile=256):
    tops, rows, width = q.shape; heads = width // HD
    by_head, two, stat = prompt_specs(tops, rows)
    return pl.pallas_call(functools.partial(prompt_bwd, tile), grid=(heads,), in_specs=[two, by_head, by_head, two, stat], out_specs=[two, by_head, by_head],
        out_shape=[jax.ShapeDtypeStruct(q.shape, BF16)] + [jax.ShapeDtypeStruct(k.shape, F32)]*2,
        compiler_params=kernel_params(1, 48), cost_estimate=cost(tops, rows, rows//2, width, 3), name="attend_prompt_back")(q, k, v, do, lse)

def attend_cont_back(q, kp, vp, k, v, do, lse, dkp, dvp, length):
    tops, rows, width = q.shape; heads = width // HD; size = 2*length
    keys, own, two, stat = cont_specs(tops, kp.shape[0], size)
    return pl.pallas_call(functools.partial(cont_bwd, length), grid=(heads, rows//size), in_specs=[two, keys, keys, own, own, two, stat, keys, keys], out_specs=[two, keys, keys, own, own],
        out_shape=[jax.ShapeDtypeStruct(m.shape, BF16) for m in (q, kp, kp, k, k)], scratch_shapes=[pltpu.VMEM((kp.shape[0], HD), F32)]*2,
        compiler_params=kernel_params(2, 48), cost_estimate=cost(tops, rows, kp.shape[0], width, 3), name="attend_cont_back")(q, kp, vp, k, v, do, lse, dkp, dvp)


def on_device(
    prompt_in,
    cont_in,
    cotan_prompt,
    cotan_cont,
    routes_attn_p,
    routes_attn_c,
    routes_ffn_p,
    routes_ffn_c,
    adapter_pick,
    norm_gains,
    router_attn,
    router_ffn,
    w_kv,
    w_query,
    w_out,
    w_gate_up,
    w_down,
    ada_in,
    ada_out,
    ada_down,
    ada_ffn,
):
    features = prompt_in.shape[2]
    n_attn = w_query.shape[0]
    n_ffn = w_down.shape[0]
    shards = lax.axis_size("shard")
    reps = lax.axis_size("rep")
    rep_id = lax.axis_index("rep")
    shard_id = lax.axis_index("shard")
    hops = range(1, shards)
    cont_len = cont_in.shape[2]
    sizes = (prompt_in.shape[1], cont_in.shape[1] * cont_len)
    width = w_kv.shape[2]
    both = range(2)
    rank = ada_in.shape[2]
    tops = routes_attn_p.shape[2]

    def tie(values, earlier):
        return values + (earlier[(0,) * earlier.ndim] * 0).astype(values.dtype)

    def gather(values):
        return lax.all_gather(values, "shard", axis=0)

    def scatter(values):
        return lax.psum_scatter(values, "shard", scatter_dimension=0, tiled=True)

    def together(former, latter):
        both_of = [m.reshape(shards, -1, m.shape[-1]) for m in (former, latter)]
        return jnp.concatenate(both_of, axis=1).reshape(-1, former.shape[-1])

    def spread_blocks(values):
        block = lambda t: lax.dynamic_index_in_dim(values, t % shards, 0, keepdims=False)
        out = [block(shard_id)]
        for hop in hops:
            pairs = [(k, (k + hop) % shards) for k in range(shards)]
            out.append(lax.ppermute(block(shard_id + hop), "shard", pairs))
        return out

    def in_order(by_distance):
        out = []
        for t in range(shards):
            value = by_distance[0]
            for hop in hops:
                value = jnp.where((shard_id - hop) % shards == t, by_distance[hop], value)
            out.append(value)
        return out

    def cube_gather(values, axis):
        shape, bit, place = values.shape, reps // 2, axis
        while bit:
            other = lax.ppermute(values, "rep", [(k, k ^ bit) for k in range(reps)])
            high = (rep_id // bit) % 2 == 1
            values = jnp.stack(
                [jnp.where(high, other, values), jnp.where(high, values, other)], axis=place
            )
            bit, place = bit // 2, place + 1
        return values.reshape(shape[:axis] + (reps,) + shape[axis:])

    flat = lambda m: m[0].reshape(-1, m.shape[-1])
    x_own = [flat(prompt_in), flat(cont_in)]
    c_own = [flat(cotan_prompt), flat(cotan_cont)]
    ra_own = [flat(routes_attn_p), flat(routes_attn_c)]
    rf_own = [flat(routes_ffn_p), flat(routes_ffn_c)]
    chosen = adapter_pick[0]
    own_in = lax.dynamic_index_in_dim(ada_in, chosen, 0, keepdims=False)
    own_out = lax.dynamic_index_in_dim(ada_out, chosen, 0, keepdims=False)
    own_down = lax.dynamic_index_in_dim(ada_down, chosen, 0, keepdims=False)
    own_ffn = lax.dynamic_index_in_dim(ada_ffn, chosen, 0, keepdims=False)
    gain_one = norm_gains[0].astype(F32)
    gain_two = norm_gains[1].astype(F32)

    factors = jnp.concatenate([own_in[:3], own_in[4:6], own_out[3:5]], axis=0)
    routes = jnp.concatenate([jnp.concatenate(m, axis=0) for m in (ra_own, rf_own)], axis=1)
    extra = jnp.concatenate([factors.reshape(-1), routes.astype(BF16).reshape(-1)])
    extra_rows = -(-extra.size // (16 * features)) * 16
    extra = jnp.pad(extra, (0, extra_rows * features - extra.size)).reshape(extra_rows, features)
    n1_own, r1, wa_own = [], [], []
    for i in both:
        normed, inverse = norm_rows(x_own[i].astype(F32), gain_one)
        normed = normed.astype(BF16)
        n1_own.append(normed)
        r1.append(inverse)
        wa_own.append(route_shares(dot32(normed, router_attn), ra_own[i]))
    sent = jnp.concatenate(n1_own + [extra], axis=0)
    load = gather(sent)
    spans = [(0, sizes[0]), sizes]
    extra = load[:, sum(sizes) :].reshape(shards, -1)
    full = extra[:, : factors.size].reshape((shards,) + factors.shape)
    full = full.transpose(1, 2, 0, 3).reshape(factors.shape[:2] + (-1,))
    a_qkv = jnp.concatenate([full[:3].reshape(3 * rank, features), router_attn.T], axis=0)
    a_ff = full[3:5].reshape(2 * rank, features)
    b_o, b_down = full[5], full[6]
    b_qkv, a_o = own_out[:3], own_in[3]
    routes = extra[:, factors.size : factors.size + routes.size].reshape((shards,) + routes.shape)
    rf = [routes[:, spans[i][0] : sum(spans[i]), tops:].astype(jnp.int32) for i in both]
    rf = [m.reshape(-1, tops) for m in rf]
    hot = [slot_onehots(rf[i], n_ffn, sizes[i]) for i in both]
    routes = jnp.pad(routes, ((0, 0), (0, 0), (0, EXT - 2 * tops)))
    piece = width // reps
    mine = lax.dynamic_index_in_dim(
        w_out.reshape(n_attn, shards, reps, piece, w_out.shape[2]), rep_id, 2, keepdims=False
    )
    turned = spread_blocks(tie(mine.transpose(1, 0, 2, 3), sent))
    turned = jnp.concatenate(in_order(turned), axis=2)
    w_o = cube_gather(turned, 1).reshape(n_attn, width, features)

    q, k, v, low1 = [None, None], [None, None], [None, None], [None, None]
    for i in both:
        q[i], k[i], v[i], low1[i] = qkv_call(load, routes, spans[i], tops, w_query, w_kv, a_qkv, b_qkv)
    o, lse = [None, None], [None, None]
    o[0], lse[0] = attend_prompt(q[0], k[0], v[0])
    c_load = [gather(tie(c_own[0], load))]
    partial = [tie(out_call(low1[0], sizes[0], o[0], w_o, a_o, b_o), c_load[0])]
    o[1], lse[1] = attend_cont(q[1], k[0], v[0], k[1], v[1], cont_len, partial[0])
    partial.append(out_call(low1[1], sizes[1], o[1], w_o, a_o, b_o))
    blank = jnp.zeros((2 * rank, own_down.shape[1]), BF16)
    fac_gu = [twice(own_ffn[0]), blank], [blank, twice(own_ffn[1])]
    fac_gu = jnp.stack([jnp.concatenate(m + [blank] * (EXT // (2 * rank) - 2), axis=0) for m in fac_gu])
    fac_d = jnp.concatenate([twice(own_down)] + [blank] * (EXT // (2 * rank) - 1), axis=0).T
    half = n_ffn // 2
    y_slots, dx, sums = [[], []], [[], []], []

    def run_experts(i, part, earlier):
        one, two, three = ffn_call(
            hot[i],
            n2[i],
            c_load[i],
            w_gate_up,
            w_down,
            fac_gu,
            fac_d,
            rank,
            earlier,
            part * half,
            half,
        )
        y_slots[i].append(one)
        dx[i].append(two)
        sums.append(three)

    def beside_low(rows):
        low = split_low(dot_nt(rows.reshape(-1, features), b_down))
        return with_ext(rows.reshape(-1, features), low).reshape(shards, -1, features + EXT)

    h1, n2_own, r2, wf_own, n2 = [], [], [], [], []
    for i in both:
        if i:
            partial[1] = tie(partial[1], n2[0])
            c_load[0] = beside_low(c_load[0])
            run_experts(0, 0, partial[1])
        hidden = x_own[i].astype(F32) + scatter(partial[i]).astype(F32)
        normed, inverse = norm_rows(hidden, gain_two)
        normed = normed.astype(BF16)
        h1.append(hidden)
        r2.append(inverse)
        n2_own.append(normed)
        wf_own.append(route_shares(dot32(normed, router_ffn), rf_own[i]))
        by_expert = jnp.sum(wf_own[i][:, :, None] * hits(rf_own[i], n_ffn), axis=1)
        low = dot_nt(normed, a_ff)
        columns = split_low(low[:, :rank]) + split_low(low[:, rank:]) + split_low(by_expert)
        n2_sent = with_ext(normed, columns)
        n2_sent = tie(n2_sent, dx[0][0] if i else partial[1])
        n2.append(gather(n2_sent))
    c_last = tie(c_own[1], n2_sent)
    c_load.append(gather(c_last))
    c_load[1] = beside_low(c_load[1])

    dh1, dh_sent, dh_load, d_partial, y_partial, y_own = [], [], [], [], [], []
    g_a_ff, g_b_down = [], []

    def sum_rows(i):
        lows = (0, 2 * rank)
        out, part = rows_call(hot[i], dx[i], n2[i], a_ff, lows, True, fac_d)
        g_a_ff.append(part)
        d_partial.append(tie(out, dh_load[0]) if i else out)
        out, part = rows_call(hot[i], y_slots[i], c_load[i], b_down, (0,), False, out)
        g_b_down.append(part)
        y_partial.append(out)

    def send_back(i, earlier):
        rows = scatter(d_partial[i])
        d_rows, ext = rows[:, :features].astype(F32), rows[:, features:]
        dw_own = ext[:, None, 4 * rank : 4 * rank + n_ffn].astype(F32)
        dw_top = jnp.sum(hits(rf_own[i], n_ffn) * dw_own, axis=2)
        d_logits = shares_back(wf_own[i], rf_own[i], n_ffn, dw_top)
        d_rows = d_rows + exact_mm(d_logits, router_ffn.astype(F32).T)
        dh1.append(c_own[i].astype(F32) + norm_back(h1[i], r2[i], gain_two, d_rows))
        dh_sent.append(tie(dh1[i], earlier).astype(BF16))
        dh_load.append(gather(dh_sent[i]))

    run_experts(0, 1, c_last)
    sum_rows(0)
    run_experts(1, 0, y_partial[0])
    send_back(0, dx[1][0])
    run_experts(1, 1, dh_sent[0])
    sum_rows(1)

    do, dwa, dq, dk, dv = ([None, None] for _ in range(5))
    g_a_o = jnp.zeros(a_o.shape, F32)
    g_b_o = jnp.zeros(b_o.shape, F32)
    for i in both:
        if i:
            send_back(1, dq[0])
        do[i], dwa[i], part_a, part_b = out_back_call(
            low1[i], sizes[i], dh_load[i], o[i], w_o, a_o, b_o
        )
        g_a_o, g_b_o = g_a_o + part_a, g_b_o + part_b
        if i:
            dq[1], dk[0], dv[0], dk[1], dv[1] = attend_cont_back(
                q[1], k[0], v[0], k[1], v[1], do[1], lse[1], dkp, dvp, cont_len
            )
        else:
            dq[0], dkp, dvp = attend_prompt_back(q[0], k[0], v[0], do[0], lse[0])
    y_own = scatter(tie(together(*y_partial), dh_load[1]))
    y_own = [y_own[span[0] : sum(span)] for span in spans]
    outs = [(h1[i] + y_own[i].astype(F32)).astype(BF16) for i in both]
    g_units, g_a_ff, g_b_down = sum(sums), sum(g_a_ff), sum(g_b_down)

    g_a_qkv = jnp.zeros((3 * rank, features), F32)
    g_b_qkv = jnp.zeros(b_qkv.shape, F32)
    grads, back = [], []
    earlier = ()
    dw_own = spread_blocks(together(*dwa).reshape(shards, -1, EXT))
    dw_own = sum(m[:, :tops].astype(F32) for m in dw_own)
    for i in both:
        rows, part_a, part_b = qkv_back_call(
            load,
            spans[i],
            dq[i],
            dk[i],
            dv[i],
            low1[i],
            w_query,
            w_kv,
            b_qkv,
            a_qkv[: 3 * rank],
            earlier,
        )
        earlier = (rows,)
        g_a_qkv, g_b_qkv = g_a_qkv + part_a, g_b_qkv + part_b
        back.append(rows)
    back = scatter(tie(together(*back), y_own[0]))
    for i in both:
        d_rows = back[spans[i][0] : sum(spans[i])].astype(F32)
        d_logits = shares_back(wa_own[i], ra_own[i], n_attn, dw_own[spans[i][0] : sum(spans[i])])
        d_rows = d_rows + exact_mm(d_logits, router_attn.astype(F32).T)
        grads.append(dh1[i] + norm_back(x_own[i].astype(F32), r1[i], gain_one, d_rows))
    adapters = ada_in.shape[0]
    pick_lines = jnp.broadcast_to(adapter_pick.astype(BF16)[:, None], (16, 128))

    partial = jnp.concatenate([g_a_qkv, g_a_ff, g_b_o, g_b_down], axis=0).astype(BF16)
    partial = partial.reshape(-1, shards, width).transpose(1, 0, 2)
    summed = sum(m.astype(F32) for m in spread_blocks(partial)).reshape(-1, rank, width)
    grads_own = [summed[:3], g_a_o[None], summed[3:5], g_b_qkv, summed[5:], g_units]
    lines = [g.astype(BF16).reshape(-1, 128) for g in grads_own]
    every = cube_gather(jnp.concatenate([pick_lines] + lines, axis=0), 0)
    picks = every[:, 0, 0].astype(F32)
    by_adapter = (picks[None, :] == jnp.arange(adapters, dtype=F32)[:, None]).astype(F32)
    total = jnp.sum(by_adapter[:, :, None, None] * every.astype(F32)[None], axis=1)
    out, start = [], pick_lines.shape[0]
    for line, grad in zip(lines, grads_own):
        out.append(total[:, start : start + line.shape[0]].reshape((adapters,) + grad.shape))
        start += line.shape[0]
    g_in = jnp.concatenate(out[:3], axis=1)
    g_out = jnp.concatenate(out[3:5], axis=1)

    shape_c = (1,) + cont_in.shape[1:]
    return (
        outs[0][None],
        outs[1].reshape(shape_c),
        grads[0][None],
        grads[1].reshape(shape_c),
        g_in,
        g_out,
        out[5][:, 2],
        out[5][:, :2],
    )


def solution(mesh):
    rows = (P("rep", "shard", None), P("rep", "shard", None, None))
    last = (
        P(None, None, None, "shard"),
        P(None, None, None, "shard"),
        P(None, None, "shard"),
        P(None, None, None, "shard"),
    )
    in_specs = (
        rows * 4
        + (P("rep"), P(), P(), P())
        + (P(None, None, "shard"),) * 3
        + (P(None, None, None, "shard"), P(None, "shard", None))
        + last
    )
    return jax.shard_map(
        on_device, mesh=mesh, in_specs=in_specs, out_specs=rows * 2 + last, check_vma=False
    )
```

```python
import functools

import jax
import jax.numpy as jnp
from jax import lax
from jax.experimental import pallas as pl
from jax.experimental.pallas import tpu as pltpu
from jax.sharding import PartitionSpec as P

HD = 128
SCALE = HD**-0.5
EPSILON = 1e-05
HIGHEST = lax.Precision.HIGHEST
F32 = jnp.float32
BF16 = jnp.bfloat16
EXT = 128


def dot32(former, latter):
    return jnp.dot(former, latter, preferred_element_type=F32)


def dot_nt(former, latter):
    return lax.dot_general(former, latter, (((1,), (1,)), ((), ())), preferred_element_type=F32)


def dot_tn(former, latter):
    return lax.dot_general(former, latter, (((0,), (0,)), ((), ())), preferred_element_type=F32)


def exact_mm(former, latter):
    return jnp.dot(former, latter, precision=HIGHEST)


def split_low(values):
    high = values.astype(BF16)
    return [high, (values - high.astype(F32)).astype(BF16)]


def twice(values):
    return jnp.concatenate([values, values], axis=0)


def norm_rows(values, scaling):
    inverse = lax.rsqrt(jnp.mean(values * values, axis=-1, keepdims=True) + EPSILON)
    return (values * inverse * scaling, inverse)


def norm_back(values, inverse, scaling, upstream):
    weighted = upstream * scaling
    inner_mean = jnp.mean(weighted * values, axis=-1, keepdims=True)
    return inverse * weighted - values * (inverse * inverse * inverse) * inner_mean


def capacity(block_rows, experts, top_count):
    return min(block_rows, ((block_rows * top_count + experts - 1) // experts + 7) // 8 * 8 + 8)


def hits(routes, experts):
    labels = jnp.arange(experts, dtype=jnp.int32)
    return (routes[:, :, None] == labels[None, None, :]).astype(F32)


def slot_onehots(routes, experts, block):
    rows, top_count = routes.shape
    slot_cap = capacity(block, experts, top_count)
    member = jnp.sum(hits(routes, experts), axis=1).reshape(-1, 2, block, experts)
    place = jnp.arange(block, dtype=jnp.int32)
    before = (place[None, :] < place[:, None]).astype(BF16)
    ranked = jnp.einsum("rq,phqe->phre", before, member.astype(BF16), preferred_element_type=F32)
    ranked = ranked + jnp.arange(2, dtype=F32)[None, :, None, None] * slot_cap
    slot_of = jnp.where(member > 0, ranked, -1.0).reshape(-1, 2 * block, experts)
    slots = jnp.arange(2 * slot_cap, dtype=F32)
    return (slot_of.transpose(2, 0, 1)[:, :, None, :] == slots[None, None, :, None]).astype(BF16)


def route_shares(logits, routes):
    chosen = jnp.einsum("rte,re->rt", hits(routes, logits.shape[1]), logits, precision=HIGHEST)
    return jax.nn.softmax(chosen, axis=-1)


def shares_back(shares, routes, experts, d_shares):
    d_chosen = shares * (d_shares - jnp.sum(shares * d_shares, axis=-1, keepdims=True))
    return jnp.sum(d_chosen[:, :, None] * hits(routes, experts), axis=1)


def with_ext(rows, columns):
    used = sum(c.shape[1] for c in columns)
    columns = [c.astype(BF16) for c in columns]
    blank = jnp.zeros((rows.shape[0], EXT - used), BF16)
    return jnp.concatenate([rows.astype(BF16)] + columns + [blank], axis=1)


def whole(*shape):
    return pl.BlockSpec(
        shape, lambda *ids: (0,) * len(shape), pipeline_mode=pl.Buffered(buffer_count=1)
    )


def anywhere():
    return pl.BlockSpec(memory_space=pl.ANY)


def kernel_params(dims, mib):
    return pltpu.CompilerParams(
        dimension_semantics=("arbitrary",) * dims, vmem_limit_bytes=mib * 2**20
    )


def pair_rows(ref, span):
    start, rows = span
    return ref[:, start : start + rows, :].reshape(2 * rows, ref.shape[2])


def ext_choice(ext, tops, experts, rank):
    ext = ext[...].astype(F32)
    at = 3 * rank
    shares = [ext[:, at + t : at + t + 1] + ext[:, at + tops + t : at + tops + t + 1] for t in range(tops)]
    at = at + 2 * tops
    chosen = [[ext[:, at + t : at + t + 1] == e for e in range(experts)] for t in range(tops)]
    return shares, chosen


def qkv_kernel(span, tops, rank, load, routes, w_q, w_kv, fac_a, fac_b, q, k, v, low_out):
    features = w_q.shape[1]
    experts = w_q.shape[0]
    rows = span[1]
    block = pair_rows(load, span)
    n1 = block
    route = pair_rows(routes, span)[:, :tops].astype(F32)
    chosen = [[route[:, t : t + 1] == e for e in range(experts)] for t in range(tops)]
    low = dot_nt(n1, fac_a[...])
    logits = [
        sum(jnp.where(chosen[t][e], low[:, 3 * rank + e : 3 * rank + e + 1], 0.0) for e in range(experts))
        for t in range(tops)
    ]
    peak = functools.reduce(jnp.maximum, logits)
    shares = [jnp.exp(m - peak) for m in logits]
    total = sum(shares)
    shares = split_low(jnp.concatenate([m / total for m in shares], axis=1))
    low_out[...] = jnp.concatenate(
        [low[:, : 3 * rank].astype(BF16)]
        + shares
        + [route.astype(BF16), jnp.zeros((2 * rows, EXT - 3 * rank - 3 * tops), BF16)],
        axis=1,
    )
    shift = []
    for j in range(3):
        wide = jnp.concatenate(split_low(low[:, rank * j : rank * (j + 1)]), axis=1)
        shift.append(dot32(wide, twice(fac_b[j])))
    k[...] = (dot32(n1, w_kv[0]) + shift[1]).astype(BF16)
    v[...] = (dot32(n1, w_kv[1]) + shift[2]).astype(BF16)
    picked = [shift[0]] * tops
    for e in range(experts):
        here = dot32(n1, w_q[e])
        for t in range(tops):
            picked[t] = picked[t] + jnp.where(chosen[t][e], here, 0.0)
    for t in range(tops):
        q[t] = picked[t].astype(BF16)


def qkv_call(load, routes, span, tops, w_q, w_kv, fac_a, fac_b):
    shards, held, wide = load.shape
    rows = span[1]
    width = w_q.shape[2]
    total = shards * rows
    rank = fac_b.shape[1]
    out = lambda n: pl.BlockSpec((2 * rows, n), lambda p: (p, 0))
    return pl.pallas_call(
        functools.partial(qkv_kernel, span, tops, rank),
        grid=(shards // 2,),
        in_specs=[
            pl.BlockSpec((2, held, wide), lambda p: (p, 0, 0)),
            pl.BlockSpec((2,) + routes.shape[1:], lambda p: (p, 0, 0)),
            whole(*w_q.shape),
            whole(*w_kv.shape),
            whole(*fac_a.shape),
            whole(*fac_b.shape),
        ],
        out_specs=[
            pl.BlockSpec((tops, 2 * rows, width), lambda p: (0, p, 0)),
            out(width),
            out(width),
            out(EXT),
        ],
        out_shape=[
            jax.ShapeDtypeStruct((tops, total, width), BF16),
            jax.ShapeDtypeStruct((total, width), BF16),
            jax.ShapeDtypeStruct((total, width), BF16),
            jax.ShapeDtypeStruct((total, EXT), BF16),
        ],
        compiler_params=kernel_params(1, 56),
        cost_estimate=pl.CostEstimate(
            flops=2 * total * w_q.shape[1] * width * (w_q.shape[0] + 2),
            bytes_accessed=2 * (w_q.size + w_kv.size + load.size),
            transcendentals=0,
        ),
        name="qkv",
    )(load, routes, w_q, w_kv, fac_a, fac_b)


def out_kernel(tops, ext, o, w_o, fac_a, fac_b, out):
    experts = w_o.shape[0]
    shares, chosen = ext_choice(ext, tops, experts, fac_a.shape[0])
    parts = [o[t].astype(F32) * shares[t] for t in range(tops)]
    low = dot_nt(sum(parts).astype(BF16), fac_a[...])
    total = dot32(jnp.concatenate(split_low(low), axis=1), twice(fac_b[...]))
    for e in range(experts):
        here = sum(jnp.where(chosen[t][e], parts[t], 0.0) for t in range(tops)).astype(BF16)
        total = total + dot32(here, w_o[e])
    out[...] = total.astype(BF16)


def out_call(ext, rows, o, w_o, fac_a, fac_b):
    tops, total, width = o.shape
    features = w_o.shape[2]
    return pl.pallas_call(
        functools.partial(out_kernel, tops),
        grid=(total // (2 * rows),),
        in_specs=[
            pl.BlockSpec((2 * rows, EXT), lambda p: (p, 0)),
            pl.BlockSpec((tops, 2 * rows, width), lambda p: (0, p, 0)),
            whole(*w_o.shape),
            whole(*fac_a.shape),
            whole(*fac_b.shape),
        ],
        out_specs=pl.BlockSpec((2 * rows, features), lambda p: (p, 0)),
        out_shape=jax.ShapeDtypeStruct((total, features), BF16),
        compiler_params=kernel_params(1, 56),
        cost_estimate=pl.CostEstimate(
            flops=2 * total * w_o.size,
            bytes_accessed=2 * (w_o.size + o.size + total * features),
            transcendentals=0,
        ),
        name="project_out",
    )(ext, o, w_o, fac_a, fac_b)


def out_back_kernel(tops, ext, dh, o, w_o, fac_a, fac_b, do, dw, grad_a, grad_b):
    experts = w_o.shape[0]
    shares, chosen = ext_choice(ext, tops, experts, fac_a.shape[0])
    block = dh[...].reshape(-1, dh.shape[2])
    rows = block.shape[0]
    low = split_low(dot_nt(block, fac_b[...]))
    shift = dot32(jnp.concatenate(low, axis=1), twice(fac_a[...]))
    picked = [shift] * tops
    for e in range(experts):
        here = dot_nt(block, w_o[e])
        for t in range(tops):
            picked[t] = picked[t] + jnp.where(chosen[t][e], here, 0.0)
    lane = lax.broadcasted_iota(jnp.int32, (rows, EXT), 1)
    back = jnp.zeros((rows, EXT), F32)
    total = None
    for t in range(tops):
        value = o[t].astype(F32)
        back = back + jnp.where(lane == t, jnp.sum(picked[t] * value, axis=1, keepdims=True), 0.0)
        do[t] = (picked[t] * shares[t]).astype(BF16)
        value = value * shares[t]
        total = value if total is None else total + value
    dw[...] = back.astype(BF16)
    total = total.astype(BF16)

    @pl.when(pl.program_id(0) == 0)
    def _():
        grad_a[...] = jnp.zeros_like(grad_a)
        grad_b[...] = jnp.zeros_like(grad_b)

    grad_a[...] += dot_tn(low[0], total)
    grad_b[...] += dot_tn(dot_nt(total, fac_a[...]).astype(BF16), block)


def out_back_call(ext, rows, dh, o, w_o, fac_a, fac_b):
    tops, total, width = o.shape
    rank, features = fac_b.shape
    two = pl.BlockSpec((tops, 2 * rows, width), lambda p: (0, p, 0))
    row = pl.BlockSpec((2 * rows, EXT), lambda p: (p, 0))
    return pl.pallas_call(
        functools.partial(out_back_kernel, tops),
        grid=(total // (2 * rows),),
        in_specs=[
            row,
            pl.BlockSpec((2,) + dh.shape[1:], lambda p: (p, 0, 0)),
            two,
            whole(*w_o.shape),
            whole(*fac_a.shape),
            whole(*fac_b.shape),
        ],
        out_specs=[
            two,
            row,
            pl.BlockSpec((rank, width), lambda p: (0, 0)),
            pl.BlockSpec((rank, features), lambda p: (0, 0)),
        ],
        out_shape=[
            jax.ShapeDtypeStruct(o.shape, BF16),
            jax.ShapeDtypeStruct((total, EXT), BF16),
            jax.ShapeDtypeStruct((rank, width), F32),
            jax.ShapeDtypeStruct((rank, features), F32),
        ],
        compiler_params=kernel_params(1, 56),
        cost_estimate=pl.CostEstimate(
            flops=2 * total * w_o.size,
            bytes_accessed=2 * (w_o.size + 2 * o.size + total * features),
            transcendentals=0,
        ),
        name="project_out_back",
    )(ext, dh, o, w_o, fac_a, fac_b)


def qkv_back_kernel(span, tops, rank, load, dq, dk, dv, low_in, w_q, w_kv, fac_b, fac_a, out, grad_a, grad_b):
    experts, features, _ = w_q.shape
    rows = span[1]
    block = pair_rows(load, span)
    _, chosen = ext_choice(low_in, tops, experts, rank)
    total = dot_nt(dk[...], w_kv[0]) + dot_nt(dv[...], w_kv[1])
    blank = jnp.zeros(dk.shape, BF16)
    for e in range(experts):
        here = blank
        for t in range(tops):
            here = jnp.where(chosen[t][e], dq[t], here)
        total = total + dot_nt(here, w_q[e])
    dq_sum = sum(dq[t].astype(F32) for t in range(tops)).astype(BF16)
    sides = [dq_sum, dk[...], dv[...]]
    low = jnp.concatenate([dot_nt(sides[j], fac_b[j]) for j in range(3)], axis=1)
    total = total + dot32(jnp.concatenate(split_low(low), axis=1), twice(fac_a[...]))
    out[...] = total.astype(BF16)

    @pl.when(pl.program_id(0) == 0)
    def _():
        grad_a[...] = jnp.zeros_like(grad_a)
        grad_b[...] = jnp.zeros_like(grad_b)

    grad_a[...] += dot_tn(low.astype(BF16), block)
    for j in range(3):
        grad_b[j] += dot_tn(low_in[:, rank * j : rank * (j + 1)], sides[j])


def qkv_back_call(load, span, dq, dk, dv, low_in, w_q, w_kv, fac_b, fac_a, earlier):
    tops, total, width = dq.shape
    rows = span[1]
    features = w_q.shape[1]
    rank = fac_b.shape[1]
    row = lambda n: pl.BlockSpec((2 * rows, n), lambda p: (p, 0))

    def kernel(*refs):
        qkv_back_kernel(span, tops, rank, *refs[:9], *refs[9 + len(earlier) :])

    return pl.pallas_call(
        kernel,
        grid=(total // (2 * rows),),
        in_specs=[
            pl.BlockSpec((2,) + load.shape[1:], lambda p: (p, 0, 0)),
            pl.BlockSpec((tops, 2 * rows, width), lambda p: (0, p, 0)),
            row(width),
            row(width),
            row(EXT),
            whole(*w_q.shape),
            whole(*w_kv.shape),
            whole(*fac_b.shape),
            whole(*fac_a.shape),
        ]
        + [anywhere() for _ in earlier],
        out_specs=[
            row(features),
            pl.BlockSpec((3 * rank, features), lambda p: (0, 0)),
            pl.BlockSpec((3, rank, width), lambda p: (0, 0, 0)),
        ],
        out_shape=[
            jax.ShapeDtypeStruct((total, features), BF16),
            jax.ShapeDtypeStruct((3 * rank, features), F32),
            jax.ShapeDtypeStruct((3, rank, width), F32),
        ],
        compiler_params=kernel_params(1, 56),
        cost_estimate=pl.CostEstimate(
            flops=2 * total * (w_q.size + w_kv.size),
            bytes_accessed=2 * (w_q.size + w_kv.size + 2 * load.size),
            transcendentals=0,
        ),
        name="qkv_back",
    )(load, dq, dk, dv, low_in, w_q, w_kv, fac_b, fac_a, *earlier)


def ffn_tiles(units):
    if units % 128:
        return [(0, units)]
    return [(start, min(512, units - start)) for start in range(0, units, 512)]


def ffn_kernel(tiles, rank, begin, hot, n2, c, w_gu, w_d, fac_gu, fac_d, y_out, dx_out, g_out, xs, cs, acc_y, acc_d, buf_gu, buf_d, sems):
    e = pl.program_id(0)
    here = pl.num_programs(0)
    experts, _, features = w_d.shape
    count = len(tiles)
    pairs, slots, _ = hot.shape[1:]
    rows = n2.shape[1]
    total = pairs * slots
    side = pl.ds(features, EXT)

    def copies(expert, t, slot):
        start, size = tiles[t]
        cols = pl.ds(start, size)
        got = pl.ds(0, size)
        pairs_of = [
            (w_gu.at[begin + expert, 0, :, cols], buf_gu.at[slot, 0, pl.ds(0, features), got]),
            (w_gu.at[begin + expert, 1, :, cols], buf_gu.at[slot, 1, pl.ds(0, features), got]),
            (w_d.at[begin + expert, cols, :], buf_d.at[slot, got, pl.ds(0, features)]),
            (fac_gu.at[:, :, cols], buf_gu.at[slot, :, side, got]),
            (fac_d.at[cols, :], buf_d.at[slot, got, side]),
        ]
        return [pltpu.make_async_copy(*m, sems.at[slot, n]) for n, m in enumerate(pairs_of)]

    @pl.when(e == 0)
    def _():
        for m in copies(0, 0, 0):
            m.start()
        g_out[...] = jnp.zeros_like(g_out)

    for p in range(pairs):
        spot = pl.ds(p * slots, slots)
        xs[spot, :] = dot32(hot[0, p], n2[2 * p : 2 * p + 2].reshape(2 * rows, -1)).astype(BF16)
        cs[spot, :] = dot32(hot[0, p], c[2 * p : 2 * p + 2].reshape(2 * rows, -1)).astype(BF16)
    lane = lax.broadcasted_iota(jnp.int32, (total, EXT), 1)
    ext = xs[:, features:]
    mine = (lane == 4 * rank + begin + e) | (lane == 4 * rank + experts + begin + e)
    share = jnp.sum(jnp.where(mine, ext.astype(F32), 0.0), axis=1, keepdims=True)
    low = [ext[:, :rank], ext[:, 2 * rank : 3 * rank], cs[:, features : features + rank]]
    low[2] = (low[2].astype(F32) * share).astype(BF16)
    dw = None
    for t, (start, size) in enumerate(tiles):
        slot = lax.rem(e * count + t, 2)
        for m in copies(e, t, slot):
            m.wait()
        if t + 1 < count:
            for m in copies(e, t + 1, 1 - slot):
                m.start()
        else:

            @pl.when(e + 1 < here)
            def _():
                for m in copies(e + 1, 0, 1 - slot):
                    m.start()

        spot = pl.ds(0, size)
        cols = pl.ds(start, size)
        wg, wu, wd = buf_gu.at[slot, 0, :, spot], buf_gu.at[slot, 1, :, spot], buf_d.at[slot, spot, :]
        g0 = dot32(xs[...], wg[...])
        g1 = dot32(xs[...], wu[...])
        da = dot_nt(cs[...], wd[...])
        sig = 1.0 / (1.0 + jnp.exp(-g0))
        silu = g0 * sig
        act = (silu * g1).astype(BF16)
        now = jnp.sum(da * act.astype(F32), axis=1, keepdims=True)
        dw = now if dw is None else dw + now
        da = da * share
        dg0 = (da * g1 * (sig + silu * (1.0 - sig))).astype(BF16)
        dg1 = (da * silu).astype(BF16)
        g_out[0, :, cols] += dot_tn(low[0], dg0)
        g_out[1, :, cols] += dot_tn(low[1], dg1)
        g_out[2, :, cols] += dot_tn(low[2], act)
        if t == 0 and count > 1:
            acc_y[...] = dot32(act, wd[...])
            acc_d[...] = dot_nt(dg0, wg[...]) + dot_nt(dg1, wu[...])
        elif t + 1 < count:
            acc_y[...] += dot32(act, wd[...])
            acc_d[...] += dot_nt(dg0, wg[...]) + dot_nt(dg1, wu[...])
        else:
            y = dot32(act, wd[...])
            d = dot_nt(dg0, wg[...]) + dot_nt(dg1, wu[...])
            if count > 1:
                y, d = y + acc_y[...], d + acc_d[...]
            y_out[0] = (y * share).astype(BF16)
            dx_out[0] = d.astype(BF16)
            d = jnp.where(lane == 4 * rank + begin + e, dw, d[:, features:])
            dx_out[0, :, features:] = d.astype(BF16)


def ffn_call(hot, n2, c, w_gu, w_d, fac_gu, fac_d, rank, earlier, begin, experts):
    _, pairs, slots, _ = hot.shape
    total = pairs * slots
    units, features = w_d.shape[1:]
    wide = features + EXT
    tiles = ffn_tiles(units)
    widest = max(size for _, size in tiles)
    one = lambda *s: pl.BlockSpec((1,) + s, lambda e: (e,) + (0,) * len(s))

    def kernel(*refs):
        ffn_kernel(tiles, rank, begin, *refs[:7], *refs[8:])

    return pl.pallas_call(
        kernel,
        grid=(experts,),
        in_specs=[
            pl.BlockSpec((1,) + hot.shape[1:], lambda e: (begin + e, 0, 0, 0)),
            whole(*n2.shape),
            whole(*c.shape),
        ]
        + [anywhere() for _ in range(5)],
        out_specs=[
            one(total, wide),
            one(total, wide),
            pl.BlockSpec((3, rank, units), lambda e: (0, 0, 0)),
        ],
        out_shape=[
            jax.ShapeDtypeStruct((experts, total, wide), BF16),
            jax.ShapeDtypeStruct((experts, total, wide), BF16),
            jax.ShapeDtypeStruct((3, rank, units), F32),
        ],
        scratch_shapes=[
            pltpu.VMEM((total, wide), BF16),
            pltpu.VMEM((total, wide), BF16),
            pltpu.VMEM((total, wide), F32),
            pltpu.VMEM((total, wide), F32),
            pltpu.VMEM((2, 2, wide, widest), BF16),
            pltpu.VMEM((2, widest, wide), BF16),
            pltpu.SemaphoreType.DMA((2, 5)),
        ],
        compiler_params=kernel_params(1, 62),
        cost_estimate=pl.CostEstimate(
            flops=12 * experts * total * features * units,
            bytes_accessed=6 * experts * features * units + 8 * experts * total * features,
            transcendentals=experts * total * units,
        ),
        name="ffn",
    )(hot, n2, c, w_gu, w_d, fac_gu, fac_d, earlier)


def rows_call(hot, parts, source, fac, lows, keep, earlier):
    experts, pairs, slots, rows = hot.shape
    wide = parts[0].shape[2]
    rank = fac.shape[0] // len(lows)
    features = wide - EXT
    parts = [m.reshape(-1, pairs, slots, wide) for m in parts]
    by_pair = lambda n, *s: pl.BlockSpec((n, 1) + s, lambda p: (0, p, 0, 0))

    def kernel(hot, *refs):
        values, source, fac, _, out, grad = refs[: len(parts)], *refs[len(parts) :]
        total = None
        slots_of = [ref[n, 0] for ref in values for n in range(ref.shape[0])]
        for e in range(experts):
            here = dot_tn(hot[e, 0], slots_of[e])
            total = here if total is None else total + here
        low = [total[:, features + at : features + at + rank] for at in lows]
        low = split_low(jnp.concatenate(low, axis=1))
        main = total[:, :features] + dot32(jnp.concatenate(low, axis=1), twice(fac[...]))
        out[:, :features] = main.astype(BF16)
        if keep:
            out[:, features:] = total[:, features:].astype(BF16)

        @pl.when(pl.program_id(0) == 0)
        def _():
            grad[...] = jnp.zeros_like(grad)

        grad[...] += dot_tn(low[0], source[:, :, :features].reshape(rows, features))

    out_wide = wide if keep else features
    return pl.pallas_call(
        kernel,
        grid=(pairs,),
        in_specs=[by_pair(experts, slots, rows)]
        + [by_pair(m.shape[0], slots, wide) for m in parts]
        + [
            pl.BlockSpec((2,) + source.shape[1:], lambda p: (p, 0, 0)),
            whole(*fac.shape),
            anywhere(),
        ],
        out_specs=[
            pl.BlockSpec((rows, out_wide), lambda p: (p, 0)),
            pl.BlockSpec(fac.shape, lambda p: (0, 0)),
        ],
        out_shape=[
            jax.ShapeDtypeStruct((pairs * rows, out_wide), BF16),
            jax.ShapeDtypeStruct(fac.shape, F32),
        ],
        compiler_params=kernel_params(1, 56),
        cost_estimate=pl.CostEstimate(
            flops=2 * hot.size * wide,
            bytes_accessed=2 * (hot.size + experts * pairs * slots * wide),
            transcendentals=0,
        ),
        name="slots_to_rows",
    )(hot, *parts, source, fac, earlier)


def whole_rows(q):
    return q.reshape(q.shape[0]*q.shape[1], q.shape[2])

def masked_pair(q, keys, diag_keys, seen):
    far = None if keys is None else dot_nt(q, keys)
    near = jnp.where(seen, dot_nt(q, diag_keys), -1e30)
    return far, near

def soft_pair(far, near):
    top = jnp.max(near, axis=1, keepdims=True)
    if far is not None: top = jnp.maximum(top, jnp.max(far, axis=1, keepdims=True))
    p_near = jnp.exp((near - top) * SCALE)
    total = jnp.sum(p_near, axis=1, keepdims=True)
    p_far = None
    if far is not None:
        p_far = jnp.exp((far - top) * SCALE)
        total = total + jnp.sum(p_far, axis=1, keepdims=True)
    return p_far, p_near, top * SCALE + jnp.log(total), 1.0 / total

def prompt_seen(tops, size):
    r = lax.broadcasted_iota(jnp.int32, (tops, size, size), 1).reshape(tops*size, size)
    k = lax.broadcasted_iota(jnp.int32, (tops*size, size), 1)
    return k <= r

def cont_seen(tops, size, length):
    r = lax.broadcasted_iota(jnp.int32, (tops, size, size), 1).reshape(tops*size, size)
    k = lax.broadcasted_iota(jnp.int32, (tops*size, size), 1)
    own = k <= r
    for start in range(length, size, length):
        own = own & ((r < start) | (k >= start))
    return own

def forward_tile(q, far_k, far_v, near_k, near_v, seen):
    far, near = masked_pair(q, far_k, near_k, seen)
    p_far, p_near, lse, inv = soft_pair(far, near)
    o = dot32(p_near.astype(BF16), near_v)
    if far is not None: o = o + dot32(p_far.astype(BF16), far_v)
    return (o * inv).astype(BF16), lse

def prompt_fwd(tile, q, k, v, o, lse):
    tops, rows, _ = q.shape
    for start in range(0, rows, tile):
        here = pl.ds(start, tile)
        out, stat = forward_tile(whole_rows(q[:, here, :]), k[:start, :] if start else None, v[:start, :] if start else None, k[here, :], v[here, :], prompt_seen(tops, tile))
        o[:, here, :] = out.reshape(tops, tile, HD)
        lse[0, :, here, :] = stat.reshape(tops, tile, 1)

def cont_fwd(length, q, kp, vp, k, v, earlier, o, lse):
    tops, size, _ = q.shape
    out, stat = forward_tile(whole_rows(q[...]), kp[...], vp[...], k[...], v[...], cont_seen(tops, size, length))
    o[...] = out.reshape(tops, size, HD)
    lse[0] = stat.reshape(tops, size, 1)

def backward_tile(q, do, lse, far_k, far_v, near_k, near_v, seen):
    far, near = masked_pair(q, far_k, near_k, seen)
    p_near = jnp.exp(near * SCALE - lse)
    dp_near = dot_nt(do, near_v)
    delta = jnp.sum(p_near * dp_near, axis=1, keepdims=True)
    if far is not None:
        p_far = jnp.exp(far * SCALE - lse)
        dp_far = dot_nt(do, far_v)
        delta = delta + jnp.sum(p_far * dp_far, axis=1, keepdims=True)
    ds_near = (p_near * (dp_near - delta)).astype(BF16)
    dq = dot32(ds_near, near_k)
    near_grads = dot_tn(ds_near, q) * SCALE, dot_tn(p_near.astype(BF16), do)
    far_grads = None
    if far is not None:
        ds_far = (p_far * (dp_far - delta)).astype(BF16)
        dq = dq + dot32(ds_far, far_k)
        far_grads = dot_tn(ds_far, q) * SCALE, dot_tn(p_far.astype(BF16), do)
    return (dq * SCALE).astype(BF16), far_grads, near_grads

def prompt_bwd(tile, q, k, v, do, lse, dq, dk, dv):
    tops, rows, _ = q.shape
    for start in range(0, rows, tile):
        here = pl.ds(start, tile)
        out, far, near = backward_tile(whole_rows(q[:, here, :]), whole_rows(do[:, here, :]), lse[0, :, here, :].reshape(tops*tile, 1),
            k[:start, :] if start else None, v[:start, :] if start else None, k[here, :], v[here, :], prompt_seen(tops, tile))
        dq[:, here, :] = out.reshape(tops, tile, HD)
        dk[here, :], dv[here, :] = near
        if start:
            dk[:start, :] += far[0]
            dv[:start, :] += far[1]

def cont_bwd(length, q, kp, vp, k, v, do, lse, dkp_in, dvp_in, dq, dkp, dvp, dk, dv, acc_k, acc_v):
    tops, size, _ = q.shape
    step = pl.program_id(1)
    @pl.when(step == 0)
    def _():
        acc_k[...] = dkp_in[...]
        acc_v[...] = dvp_in[...]
    out, far, near = backward_tile(whole_rows(q[...]), whole_rows(do[...]), lse[0].reshape(tops*size, 1), kp[...], vp[...], k[...], v[...], cont_seen(tops, size, length))
    dq[...] = out.reshape(tops, size, HD)
    dk[...], dv[...] = near[0].astype(BF16), near[1].astype(BF16)
    acc_k[...] += far[0]
    acc_v[...] += far[1]
    @pl.when(step == pl.num_programs(1) - 1)
    def _():
        dkp[...] = acc_k[...].astype(BF16)
        dvp[...] = acc_v[...].astype(BF16)

def cost(tops, rows, keys, width, products):
    return pl.CostEstimate(flops=4*tops*rows*keys*width*products, bytes_accessed=8*rows*width*tops, transcendentals=tops*rows*keys*width//HD)

def prompt_specs(tops, rows):
    by_head = pl.BlockSpec((rows, HD), lambda h: (0, h))
    two = pl.BlockSpec((tops, rows, HD), lambda h: (0, 0, h))
    stat = pl.BlockSpec((1, tops, rows, 1), lambda h: (h, 0, 0, 0))
    return by_head, two, stat

def cont_specs(tops, prompt, size):
    keys = pl.BlockSpec((prompt, HD), lambda h, i: (0, h))
    own = pl.BlockSpec((size, HD), lambda h, i: (i, h))
    two = pl.BlockSpec((tops, size, HD), lambda h, i: (0, i, h))
    stat = pl.BlockSpec((1, tops, size, 1), lambda h, i: (h, 0, i, 0))
    return keys, own, two, stat

def attend_prompt(q, k, v, tile=256):
    tops, rows, width = q.shape; heads = width // HD
    by_head, two, stat = prompt_specs(tops, rows)
    return pl.pallas_call(functools.partial(prompt_fwd, tile), grid=(heads,), in_specs=[two, by_head, by_head], out_specs=[two, stat],
        out_shape=[jax.ShapeDtypeStruct(q.shape, BF16), jax.ShapeDtypeStruct((heads, tops, rows, 1), F32)],
        compiler_params=kernel_params(1, 48), cost_estimate=cost(tops, rows, rows//2, width, 1), name="attend_prompt")(q, k, v)

def attend_cont(q, kp, vp, k, v, length, earlier):
    tops, rows, width = q.shape; heads = width // HD; size = 2*length
    keys, own, two, stat = cont_specs(tops, kp.shape[0], size)
    return pl.pallas_call(functools.partial(cont_fwd, length), grid=(heads, rows//size), in_specs=[two, keys, keys, own, own, anywhere()], out_specs=[two, stat],
        out_shape=[jax.ShapeDtypeStruct(q.shape, BF16), jax.ShapeDtypeStruct((heads, tops, rows, 1), F32)],
        compiler_params=kernel_params(2, 48), cost_estimate=cost(tops, rows, kp.shape[0], width, 1), name="attend_cont")(q, kp, vp, k, v, earlier)

def attend_prompt_back(q, k, v, do, lse, tile=256):
    tops, rows, width = q.shape; heads = width // HD
    by_head, two, stat = prompt_specs(tops, rows)
    return pl.pallas_call(functools.partial(prompt_bwd, tile), grid=(heads,), in_specs=[two, by_head, by_head, two, stat], out_specs=[two, by_head, by_head],
        out_shape=[jax.ShapeDtypeStruct(q.shape, BF16)] + [jax.ShapeDtypeStruct(k.shape, F32)]*2,
        compiler_params=kernel_params(1, 48), cost_estimate=cost(tops, rows, rows//2, width, 3), name="attend_prompt_back")(q, k, v, do, lse)

def attend_cont_back(q, kp, vp, k, v, do, lse, dkp, dvp, length):
    tops, rows, width = q.shape; heads = width // HD; size = 2*length
    keys, own, two, stat = cont_specs(tops, kp.shape[0], size)
    return pl.pallas_call(functools.partial(cont_bwd, length), grid=(heads, rows//size), in_specs=[two, keys, keys, own, own, two, stat, keys, keys], out_specs=[two, keys, keys, own, own],
        out_shape=[jax.ShapeDtypeStruct(m.shape, BF16) for m in (q, kp, kp, k, k)], scratch_shapes=[pltpu.VMEM((kp.shape[0], HD), F32)]*2,
        compiler_params=kernel_params(2, 48), cost_estimate=cost(tops, rows, kp.shape[0], width, 3), name="attend_cont_back")(q, kp, vp, k, v, do, lse, dkp, dvp)


def on_device(
    prompt_in,
    cont_in,
    cotan_prompt,
    cotan_cont,
    routes_attn_p,
    routes_attn_c,
    routes_ffn_p,
    routes_ffn_c,
    adapter_pick,
    norm_gains,
    router_attn,
    router_ffn,
    w_kv,
    w_query,
    w_out,
    w_gate_up,
    w_down,
    ada_in,
    ada_out,
    ada_down,
    ada_ffn,
):
    features = prompt_in.shape[2]
    n_attn = w_query.shape[0]
    n_ffn = w_down.shape[0]
    shards = lax.axis_size("shard")
    reps = lax.axis_size("rep")
    rep_id = lax.axis_index("rep")
    shard_id = lax.axis_index("shard")
    hops = range(1, shards)
    cont_len = cont_in.shape[2]
    sizes = (prompt_in.shape[1], cont_in.shape[1] * cont_len)
    width = w_kv.shape[2]
    both = range(2)
    rank = ada_in.shape[2]
    tops = routes_attn_p.shape[2]

    def tie(values, earlier):
        return values + (earlier[(0,) * earlier.ndim] * 0).astype(values.dtype)

    def gather(values):
        return lax.all_gather(values, "shard", axis=0)

    def scatter(values):
        return lax.psum_scatter(values, "shard", scatter_dimension=0, tiled=True)

    def together(former, latter):
        both_of = [m.reshape(shards, -1, m.shape[-1]) for m in (former, latter)]
        return jnp.concatenate(both_of, axis=1).reshape(-1, former.shape[-1])

    def spread_blocks(values):
        block = lambda t: lax.dynamic_index_in_dim(values, t % shards, 0, keepdims=False)
        out = [block(shard_id)]
        for hop in hops:
            pairs = [(k, (k + hop) % shards) for k in range(shards)]
            out.append(lax.ppermute(block(shard_id + hop), "shard", pairs))
        return out

    def in_order(by_distance):
        out = []
        for t in range(shards):
            value = by_distance[0]
            for hop in hops:
                value = jnp.where((shard_id - hop) % shards == t, by_distance[hop], value)
            out.append(value)
        return out

    def cube_gather(values, axis):
        shape, bit, place = values.shape, reps // 2, axis
        while bit:
            other = lax.ppermute(values, "rep", [(k, k ^ bit) for k in range(reps)])
            high = (rep_id // bit) % 2 == 1
            values = jnp.stack(
                [jnp.where(high, other, values), jnp.where(high, values, other)], axis=place
            )
            bit, place = bit // 2, place + 1
        return values.reshape(shape[:axis] + (reps,) + shape[axis:])

    flat = lambda m: m[0].reshape(-1, m.shape[-1])
    x_own = [flat(prompt_in), flat(cont_in)]
    c_own = [flat(cotan_prompt), flat(cotan_cont)]
    ra_own = [flat(routes_attn_p), flat(routes_attn_c)]
    rf_own = [flat(routes_ffn_p), flat(routes_ffn_c)]
    chosen = adapter_pick[0]
    own_in = lax.dynamic_index_in_dim(ada_in, chosen, 0, keepdims=False)
    own_out = lax.dynamic_index_in_dim(ada_out, chosen, 0, keepdims=False)
    own_down = lax.dynamic_index_in_dim(ada_down, chosen, 0, keepdims=False)
    own_ffn = lax.dynamic_index_in_dim(ada_ffn, chosen, 0, keepdims=False)
    gain_one = norm_gains[0].astype(F32)
    gain_two = norm_gains[1].astype(F32)

    factors = jnp.concatenate([own_in[:3], own_in[4:6], own_out[3:5]], axis=0)
    routes = jnp.concatenate([jnp.concatenate(m, axis=0) for m in (ra_own, rf_own)], axis=1)
    extra = jnp.concatenate([factors.reshape(-1), routes.astype(BF16).reshape(-1)])
    extra_rows = -(-extra.size // (16 * features)) * 16
    extra = jnp.pad(extra, (0, extra_rows * features - extra.size)).reshape(extra_rows, features)
    n1_own, r1, wa_own = [], [], []
    for i in both:
        normed, inverse = norm_rows(x_own[i].astype(F32), gain_one)
        normed = normed.astype(BF16)
        n1_own.append(normed)
        r1.append(inverse)
        wa_own.append(route_shares(dot32(normed, router_attn), ra_own[i]))
    sent = jnp.concatenate(n1_own + [extra], axis=0)
    load = gather(sent)
    spans = [(0, sizes[0]), sizes]
    extra = load[:, sum(sizes) :].reshape(shards, -1)
    full = extra[:, : factors.size].reshape((shards,) + factors.shape)
    full = full.transpose(1, 2, 0, 3).reshape(factors.shape[:2] + (-1,))
    a_qkv = jnp.concatenate([full[:3].reshape(3 * rank, features), router_attn.T], axis=0)
    a_ff = full[3:5].reshape(2 * rank, features)
    b_o, b_down = full[5], full[6]
    b_qkv, a_o = own_out[:3], own_in[3]
    routes = extra[:, factors.size : factors.size + routes.size].reshape((shards,) + routes.shape)
    rf = [routes[:, spans[i][0] : sum(spans[i]), tops:].astype(jnp.int32) for i in both]
    rf = [m.reshape(-1, tops) for m in rf]
    hot = [slot_onehots(rf[i], n_ffn, sizes[i]) for i in both]
    routes = jnp.pad(routes, ((0, 0), (0, 0), (0, EXT - 2 * tops)))
    piece = width // reps
    mine = lax.dynamic_index_in_dim(
        w_out.reshape(n_attn, shards, reps, piece, w_out.shape[2]), rep_id, 2, keepdims=False
    )
    turned = spread_blocks(tie(mine.transpose(1, 0, 2, 3), sent))
    turned = jnp.concatenate(in_order(turned), axis=2)
    w_o = cube_gather(turned, 1).reshape(n_attn, width, features)

    q, k, v, low1 = [None, None], [None, None], [None, None], [None, None]
    for i in both:
        q[i], k[i], v[i], low1[i] = qkv_call(load, routes, spans[i], tops, w_query, w_kv, a_qkv, b_qkv)
    o, lse = [None, None], [None, None]
    o[0], lse[0] = attend_prompt(q[0], k[0], v[0])
    c_load = [gather(tie(c_own[0], load))]
    partial = [tie(out_call(low1[0], sizes[0], o[0], w_o, a_o, b_o), c_load[0])]
    o[1], lse[1] = attend_cont(q[1], k[0], v[0], k[1], v[1], cont_len, partial[0])
    partial.append(out_call(low1[1], sizes[1], o[1], w_o, a_o, b_o))
    blank = jnp.zeros((2 * rank, own_down.shape[1]), BF16)
    fac_gu = [twice(own_ffn[0]), blank], [blank, twice(own_ffn[1])]
    fac_gu = jnp.stack([jnp.concatenate(m + [blank] * (EXT // (2 * rank) - 2), axis=0) for m in fac_gu])
    fac_d = jnp.concatenate([twice(own_down)] + [blank] * (EXT // (2 * rank) - 1), axis=0).T
    half = n_ffn // 2
    ahead = max(1, half // 2)
    y_slots, dx, sums = [[], []], [[], []], []

    def run_experts(i, begin, count, earlier):
        one, two, three = ffn_call(
            hot[i],
            n2[i],
            c_load[i],
            w_gate_up,
            w_down,
            fac_gu,
            fac_d,
            rank,
            earlier,
            begin,
            count,
        )
        y_slots[i].append(one)
        dx[i].append(two)
        sums.append(three)

    def beside_low(rows):
        low = split_low(dot_nt(rows.reshape(-1, features), b_down))
        return with_ext(rows.reshape(-1, features), low).reshape(shards, -1, features + EXT)

    h1, n2_own, r2, wf_own, n2 = [], [], [], [], []
    for i in both:
        if i:
            partial[1] = tie(partial[1], n2[0])
            c_load[0] = beside_low(c_load[0])
            run_experts(0, 0, ahead, partial[1])
        hidden = x_own[i].astype(F32) + scatter(partial[i]).astype(F32)
        normed, inverse = norm_rows(hidden, gain_two)
        normed = normed.astype(BF16)
        h1.append(hidden)
        r2.append(inverse)
        n2_own.append(normed)
        wf_own.append(route_shares(dot32(normed, router_ffn), rf_own[i]))
        by_expert = jnp.sum(wf_own[i][:, :, None] * hits(rf_own[i], n_ffn), axis=1)
        low = dot_nt(normed, a_ff)
        columns = split_low(low[:, :rank]) + split_low(low[:, rank:]) + split_low(by_expert)
        n2_sent = with_ext(normed, columns)
        n2_sent = tie(n2_sent, dx[0][0] if i else partial[1])
        n2.append(gather(n2_sent))
    c_last = tie(c_own[1], n2_sent)
    c_load.append(gather(c_last))
    c_load[1] = beside_low(c_load[1])

    dh1, dh_sent, dh_load, d_partial, y_partial, y_own = [], [], [], [], [], []
    g_a_ff, g_b_down = [], []

    def sum_rows(i):
        lows = (0, 2 * rank)
        out, part = rows_call(hot[i], dx[i], n2[i], a_ff, lows, True, fac_d)
        g_a_ff.append(part)
        d_partial.append(tie(out, dh_load[0]) if i else out)
        out, part = rows_call(hot[i], y_slots[i], c_load[i], b_down, (0,), False, out)
        g_b_down.append(part)
        y_partial.append(out)

    def send_back(i, earlier):
        rows = scatter(d_partial[i])
        d_rows, ext = rows[:, :features].astype(F32), rows[:, features:]
        dw_own = ext[:, None, 4 * rank : 4 * rank + n_ffn].astype(F32)
        dw_top = jnp.sum(hits(rf_own[i], n_ffn) * dw_own, axis=2)
        d_logits = shares_back(wf_own[i], rf_own[i], n_ffn, dw_top)
        d_rows = d_rows + exact_mm(d_logits, router_ffn.astype(F32).T)
        dh1.append(c_own[i].astype(F32) + norm_back(h1[i], r2[i], gain_two, d_rows))
        dh_sent.append(tie(dh1[i], earlier).astype(BF16))
        dh_load.append(gather(dh_sent[i]))

    run_experts(0, ahead, n_ffn - ahead, c_last)
    sum_rows(0)
    run_experts(1, 0, half, y_partial[0])
    send_back(0, dx[1][0])
    run_experts(1, half, n_ffn - half, dh_sent[0])
    sum_rows(1)

    do, dwa, dq, dk, dv = ([None, None] for _ in range(5))
    g_a_o = jnp.zeros(a_o.shape, F32)
    g_b_o = jnp.zeros(b_o.shape, F32)
    for i in both:
        if i:
            send_back(1, dq[0])
        do[i], dwa[i], part_a, part_b = out_back_call(
            low1[i], sizes[i], dh_load[i], o[i], w_o, a_o, b_o
        )
        g_a_o, g_b_o = g_a_o + part_a, g_b_o + part_b
        if i:
            dq[1], dk[0], dv[0], dk[1], dv[1] = attend_cont_back(
                q[1], k[0], v[0], k[1], v[1], do[1], lse[1], dkp, dvp, cont_len
            )
        else:
            dq[0], dkp, dvp = attend_prompt_back(q[0], k[0], v[0], do[0], lse[0])
    y_own = scatter(tie(together(*y_partial), dh_load[1]))
    y_own = [y_own[span[0] : sum(span)] for span in spans]
    outs = [(h1[i] + y_own[i].astype(F32)).astype(BF16) for i in both]
    g_units, g_a_ff, g_b_down = sum(sums), sum(g_a_ff), sum(g_b_down)

    g_a_qkv = jnp.zeros((3 * rank, features), F32)
    g_b_qkv = jnp.zeros(b_qkv.shape, F32)
    grads, back = [], []
    earlier = ()
    dw_own = together(*(m[:, :tops] for m in dwa)).reshape(shards, -1, tops).transpose(0, 2, 1)
    dw_own = sum(m.astype(F32) for m in spread_blocks(dw_own)).T
    for i in both:
        rows, part_a, part_b = qkv_back_call(
            load,
            spans[i],
            dq[i],
            dk[i],
            dv[i],
            low1[i],
            w_query,
            w_kv,
            b_qkv,
            a_qkv[: 3 * rank],
            earlier,
        )
        earlier = (rows,)
        g_a_qkv, g_b_qkv = g_a_qkv + part_a, g_b_qkv + part_b
        back.append(rows)
    back = scatter(tie(together(*back), y_own[0]))
    for i in both:
        d_rows = back[spans[i][0] : sum(spans[i])].astype(F32)
        d_logits = shares_back(wa_own[i], ra_own[i], n_attn, dw_own[spans[i][0] : sum(spans[i])])
        d_rows = d_rows + exact_mm(d_logits, router_attn.astype(F32).T)
        grads.append(dh1[i] + norm_back(x_own[i].astype(F32), r1[i], gain_one, d_rows))
    adapters = ada_in.shape[0]
    pick_lines = jnp.broadcast_to(adapter_pick.astype(BF16)[:, None], (16, 128))

    partial = jnp.concatenate([g_a_qkv, g_a_ff, g_b_o, g_b_down], axis=0).astype(BF16)
    partial = partial.reshape(-1, shards, width).transpose(1, 0, 2)
    summed = sum(m.astype(F32) for m in spread_blocks(partial)).reshape(-1, rank, width)
    grads_own = [summed[:3], g_a_o[None], summed[3:5], g_b_qkv, summed[5:], g_units]
    lines = [g.astype(BF16).reshape(-1, 128) for g in grads_own]
    every = cube_gather(jnp.concatenate([pick_lines] + lines, axis=0), 0)
    picks = every[:, 0, 0].astype(F32)
    by_adapter = (picks[None, :] == jnp.arange(adapters, dtype=F32)[:, None]).astype(F32)
    total = jnp.sum(by_adapter[:, :, None, None] * every.astype(F32)[None], axis=1)
    out, start = [], pick_lines.shape[0]
    for line, grad in zip(lines, grads_own):
        out.append(total[:, start : start + line.shape[0]].reshape((adapters,) + grad.shape))
        start += line.shape[0]
    g_in = jnp.concatenate(out[:3], axis=1)
    g_out = jnp.concatenate(out[3:5], axis=1)

    shape_c = (1,) + cont_in.shape[1:]
    return (
        outs[0][None],
        outs[1].reshape(shape_c),
        grads[0][None],
        grads[1].reshape(shape_c),
        g_in,
        g_out,
        out[5][:, 2],
        out[5][:, :2],
    )


def solution(mesh):
    rows = (P("rep", "shard", None), P("rep", "shard", None, None))
    last = (
        P(None, None, None, "shard"),
        P(None, None, None, "shard"),
        P(None, None, "shard"),
        P(None, None, None, "shard"),
    )
    in_specs = (
        rows * 4
        + (P("rep"), P(), P(), P())
        + (P(None, None, "shard"),) * 3
        + (P(None, None, None, "shard"), P(None, "shard", None))
        + last
    )
    return jax.shard_map(
        on_device, mesh=mesh, in_specs=in_specs, out_specs=rows * 2 + last, check_vma=False
    )
```
